32 devices in a mesh: group: 4 (over y, core), within: 8 (over z, x).
Axes of the slice: x: 2, y: 2, z: 4, core: 2. Of those that a mesh axis runs over, the one named last changes fastest.
Arguments:
- tokens: bfloat16 [4096, 2048], P(('group', 'within')), may hold values from -6 to 6
- languages: int32 [4096], P(('group', 'within')), may hold values from 0 to 99, as said below
- lang_group: int32 [100], replicated, may hold values from 0 to 3, as said below
- group_gain: float32 [4, 2048], replicated, may hold values from 0.25 to 1.75
- group_w1: bfloat16 [4, 2048, 8192], P('group', None, 'within'), may hold values from -0.125 to 0.125
- group_b1: float32 [4, 8192], P('group', 'within'), may hold values from -3 to 3
- group_w2: bfloat16 [4, 8192, 2048], P('group', 'within'), may hold values from -0.0625 to 0.0625
- group_b2: float32 [4, 2048], replicated, may hold values from -3 to 3
- shared_gain: float32 [2048], replicated, may hold values from 0.25 to 1.75
- shared_w1: bfloat16 [2048, 8192], P(None, 'group'), may hold values from -0.125 to 0.125
- shared_b1: float32 [8192], P('group'), may hold values from -3 to 3
- shared_w2: bfloat16 [8192, 2048], P('group'), may hold values from -0.0625 to 0.0625
- shared_b2: float32 [2048], replicated, may hold values from -3 to 3
Outputs:
- encoded: bfloat16 [4096, 2048], P(('group', 'within'))
The draws below stay inside these ranges and needn't reach their ends.
Inputs may be any that keep to these rules, and one draw needn't show every extreme that they name: `lang_group`: every language lies in one group and every group holds at least one language. Among the 128 tokens of one device (an aligned block), at most 48 have languages of one group, and in every block some group has exactly 48.
All inputs are finite; a program needn't handle non-finite values.
Results may differ from the reference program's by a relative error of at most 0.017.
Values may be sent and summed in bfloat16 or wider, within the bound.
A program may use at most 128 MiB of HBM per device.

```python
import jax
import jax.numpy as jnp
from jax import lax

D = 2048
FF = 8192
LANGS = 100
TOK_DEV = 128
GROUPS = 4
CAP = 48
TOKENS = 4096
N_WITHIN = 8
DEVICES = 32


def joint_draw(key):
    ordering = jax.random.permutation(jax.random.fold_in(key, 11), LANGS).astype(jnp.int32)
    lang_table = jnp.zeros((LANGS,), jnp.int32).at[ordering].set((jnp.arange(LANGS, dtype=jnp.int32) % GROUPS).astype(jnp.int32))
    num_blocks = TOKENS // TOK_DEV
    favourite = jax.random.randint(jax.random.fold_in(key, 12), (), 0, GROUPS)
    coinflip = jax.random.randint(jax.random.fold_in(key, 13), (num_blocks,), 0, 4)
    others = jax.random.randint(jax.random.fold_in(key, 14), (num_blocks,), 0, GROUPS)
    hottest = jnp.where(coinflip < 3, favourite, others).astype(jnp.int32)
    position = jnp.arange(TOK_DEV, dtype=jnp.int32)
    remaining = (hottest[:, None] + 1 + (position[None, :] - CAP) % (GROUPS - 1)) % GROUPS
    group_rows = jnp.where(position[None, :] < CAP, hottest[:, None], remaining).astype(jnp.int32)
    block_keys = jax.random.split(jax.random.fold_in(key, 15), num_blocks)
    shuffles = jax.vmap(lambda single: jax.random.permutation(single, TOK_DEV))(block_keys).astype(jnp.int32)
    group_rows = jnp.take_along_axis(group_rows, shuffles, axis=1)
    group_sizes = (LANGS - group_rows + GROUPS - 1) // GROUPS
    first_pick = jax.random.randint(jax.random.fold_in(key, 16), group_rows.shape, 0, 1048576) % group_sizes
    second_pick = jax.random.randint(jax.random.fold_in(key, 17), group_rows.shape, 0, 1048576) % group_sizes
    chosen = jnp.minimum(first_pick, second_pick)
    language_ids = ordering[group_rows + GROUPS * chosen]
    return (lang_table, language_ids.reshape(TOKENS).astype(jnp.int32))


def draw_languages(key, part):
    return joint_draw(key)[1]


def draw_lang_group(key, part):
    return joint_draw(key)[0]


def shard_levels(own_key, shape, shards, low, high):
    def one(axis_at, blocks):
        steps = jax.random.uniform(jax.random.fold_in(jax.random.fold_in(own_key, 6), axis_at), (blocks,), jnp.float32, low / len(shards), high / len(shards))
        return jnp.repeat(jnp.exp(steps), shape[axis_at] // blocks).reshape((-1,) + (1,) * (len(shape) - axis_at - 1))

    factor_of = one(*shards[0])
    for cut in shards[1:]:
        factor_of = factor_of * one(*cut)
    return factor_of


def bell_draw(rng, shape, scale, bound, shards=(), held_as=jnp.bfloat16):
    drawn = jax.random.normal(rng, shape, jnp.float32) * scale
    if len(shards) > 0:
        drawn = shard_levels(rng, shape, shards, -0.22, 0.18) * drawn
    return jnp.clip(drawn, min=-bound, max=bound).astype(held_as)


def setup_inputs(seed: int = 0) -> dict:
    key_of = jax.random.split(jax.random.key(seed), 14)
    return {
        "tokens": bell_draw(key_of[0], (TOKENS, D), 1.0, 6.0, ((0, 32),)),
        "languages": draw_languages(jax.random.fold_in(key_of[13], 71), 0),
        "lang_group": draw_lang_group(jax.random.fold_in(key_of[13], 71), 0),
        "group_gain": jnp.clip(1.0 + 0.15 * jax.random.normal(key_of[3], (GROUPS, D), jnp.float32), 0.25, 1.75),
        "group_w1": bell_draw(key_of[4], (GROUPS, D, FF), D ** -0.5, 0.125, ((0, 4), (2, 8))),
        "group_b1": bell_draw(key_of[5], (GROUPS, FF), 0.5, 3.0, ((0, 4), (1, 8)), jnp.float32),
        "group_w2": bell_draw(key_of[6], (GROUPS, FF, D), FF ** -0.5, 0.0625, ((0, 4), (1, 8))),
        "group_b2": bell_draw(key_of[7], (GROUPS, D), 0.5, 3.0, (), jnp.float32),
        "shared_gain": jnp.clip(1.0 + 0.15 * jax.random.normal(key_of[8], (D,), jnp.float32), 0.25, 1.75),
        "shared_w1": bell_draw(key_of[9], (D, FF), D ** -0.5, 0.125, ((1, 4),)),
        "shared_b1": bell_draw(key_of[10], (FF,), 0.5, 3.0, ((0, 4),), jnp.float32),
        "shared_w2": bell_draw(key_of[11], (FF, D), FF ** -0.5, 0.0625, ((0, 4),)),
        "shared_b2": bell_draw(key_of[12], (D,), 0.5, 3.0, (), jnp.float32),
    }


def layer_norm(values, gains):
    centre = lax.optimization_barrier(jnp.mean(values, axis=-1, keepdims=True))
    centred = values - centre
    spread = lax.optimization_barrier(jnp.mean(centred * centred, axis=-1, keepdims=True))
    return centred * lax.rsqrt(spread + 1e-05) * gains

def reference(tokens, languages, lang_group, group_gain, group_w1, group_b1, group_w2, group_b2, shared_gain, shared_w1, shared_b1, shared_w2, shared_b2):
    residual_in = tokens.astype(jnp.float32)
    lang_hit = (languages[:, None] == jnp.arange(LANGS, dtype=jnp.int32)[None, :]).astype(jnp.int32)
    group_of = lax.optimization_barrier(jnp.sum(lang_hit * lang_group[None, :], axis=1)).astype(jnp.int32)
    onehot = (group_of[:, None] == jnp.arange(GROUPS, dtype=jnp.int32)[None, :]).astype(jnp.int32)
    blocks = onehot.reshape(DEVICES, TOK_DEV, GROUPS)
    earlier = jnp.cumsum(blocks, axis=1) - blocks
    slot_index = lax.optimization_barrier(jnp.sum(earlier * blocks, axis=2)).reshape(TOKENS).astype(jnp.int32)
    device = (jnp.arange(TOKENS, dtype=jnp.int32) // TOK_DEV).astype(jnp.int32)
    normed = layer_norm(residual_in, group_gain[group_of]).astype(jnp.bfloat16)
    position = (device * CAP + slot_index).astype(jnp.int32)
    unit_width = FF // N_WITHIN
    group_out = jnp.zeros((TOKENS, D), jnp.bfloat16)
    for group in range(GROUPS):
        member = group_of == group
        target = jnp.where(member, position, DEVICES * CAP).astype(jnp.int32)
        buffer = jnp.zeros((DEVICES * CAP, D), jnp.bfloat16).at[target].set(normed, mode='drop')
        hidden = jax.nn.relu(jnp.dot(buffer, group_w1[group], preferred_element_type=jnp.float32) + group_b1[group]).astype(jnp.bfloat16)
        accum_sum = jnp.zeros((DEVICES * CAP, D), jnp.float32)
        for block in range(N_WITHIN):
            partial_value = jnp.dot(hidden[:, block * unit_width:(block + 1) * unit_width], group_w2[group, block * unit_width:(block + 1) * unit_width], preferred_element_type=jnp.float32)
            accum_sum = accum_sum + lax.optimization_barrier(partial_value.astype(jnp.bfloat16)).astype(jnp.float32)
        result = accum_sum.astype(jnp.bfloat16)
        fetched = result[jnp.where(member, position, 0).astype(jnp.int32)]
        group_out = jnp.where(member[:, None], fetched, group_out)
    middle = residual_in + group_out.astype(jnp.float32) + group_b2[group_of]
    shared_in = layer_norm(middle, shared_gain).astype(jnp.bfloat16)
    shared_hidden = jax.nn.relu(jnp.dot(shared_in, shared_w1, preferred_element_type=jnp.float32) + shared_b1).astype(jnp.bfloat16)
    shared_out = jnp.dot(shared_hidden, shared_w2, preferred_element_type=jnp.float32)
    return (middle + shared_out + shared_b2).astype(jnp.bfloat16)
```

```python
import functools

import jax
import jax.numpy as jnp
from jax import lax
from jax.experimental import pallas as pl
from jax.experimental.pallas import tpu as pltpu
from jax.sharding import PartitionSpec as P

MESH = pl.DeviceIdType.MESH
TILE = 256


def layer_norm(values, gains):
    centre = jnp.mean(values, axis=-1, keepdims=True)
    centred = values - centre
    spread = jnp.mean(centred * centred, axis=-1, keepdims=True)
    return centred * lax.rsqrt(spread + 1e-05) * gains


def columns(tile, size):
    return pl.ds(pl.multiple_of(tile * size, size), size)


def fused_kernel(
    cap,
    out_rows,
    back_map,
    residual,
    b1,
    gain2,
    sb1,
    sb2,
    w1_hbm,
    w2_hbm,
    sw1_hbm,
    sw2_hbm,
    encoded,
    w1,
    w2,
    sw1,
    sw2,
    rows,
    part,
    rs,
    hidden,
    ret,
    sgather,
    shidden,
    spart,
    sown,
    scross,
    ssum,
    middle,
    w_sem,
    local_sem,
    disp_send,
    disp_recv,
    g_send,
    g_recv,
    r_send,
    r_recv,
    ret_send,
    ret_recv,
    sg_send,
    sg_recv,
    sr_send,
    sr_recv,
):
    g = lax.axis_index("group")
    w = lax.axis_index("within")
    last = 7
    x, z = lax.rem(w, 2), lax.div(w, 2)
    p = z + x * (last - 2 * z)

    def device_at(q):
        q = lax.rem(q + 8, 8)
        far = lax.div(q, 4)
        return 2 * q + far * (15 - 4 * q)

    right = (g, device_at(p + 1))
    left = (g, device_at(p - 1))
    yy, core = lax.div(g, 2), lax.rem(g, 2)
    peers = [
        None,
        (2 * yy + 1 - core, w),
        (2 * (1 - yy) + core, w),
        (2 * (1 - yy) + 1 - core, w),
    ]

    loads = []
    for i, (src, dst) in enumerate(
        ((w1_hbm, w1), (w2_hbm, w2), (sw1_hbm, sw1), (sw2_hbm, sw2))
    ):
        copy = pltpu.make_async_copy(src, dst, w_sem.at[i])
        copy.start()
        loads.append(copy)
    own = pltpu.make_async_copy(
        out_rows.at[pl.ds(0, cap)], rows.at[pl.ds(0, cap)], local_sem
    )
    own.start()

    barrier = pltpu.get_barrier_semaphore()
    for device in (right, left, peers[1], peers[2], peers[3]):
        pl.semaphore_signal(barrier, inc=1, device_id=device, device_id_type=MESH)
    pl.semaphore_wait(barrier, 5)

    pending = []

    def send(src, dst, send_sem, recv_sem, device):
        copy = pltpu.make_async_remote_copy(
            src_ref=src,
            dst_ref=dst,
            send_sem=send_sem,
            recv_sem=recv_sem,
            device_id=device,
            device_id_type=MESH,
        )
        copy.start()
        pending.append(copy)
        return copy

    def chunk(slot, c):
        return pl.ds((slot * 4 + c) * cap, cap)

    dispatch = [None] * 4
    for r in (2, 3, 1):
        dispatch[r] = send(
            out_rows.at[pl.ds(r * cap, cap)],
            rows.at[chunk(0, r)],
            disp_send.at[r],
            disp_recv.at[r],
            peers[r],
        )

    def slot_of(way, s):
        return 7 if s == 4 else (0 if s == 0 else 2 * s - 1 + way)

    arrivals = {}

    def forward(way, s, c):
        slot = slot_of(way, s)
        arrivals[way, s + 1, c] = send(
            rows.at[chunk(slot, c)],
            rows.at[chunk(slot_of(way, s + 1), c)],
            g_send.at[way, s, c],
            g_recv.at[way, s + 1, c],
            right if way == 0 else left,
        )

    def first_tiles(slot, count, begin, end):
        size = count * 4 * cap

        def body(i, carry):
            cols = columns(i, TILE)
            value = jnp.dot(
                rows[pl.ds(slot * 4 * cap, size), :],
                w1[:, cols],
                preferred_element_type=jnp.float32,
            )
            hidden[pl.ds(0, size), cols] = jnp.maximum(value + b1[:, cols], 0.0).astype(
                jnp.bfloat16
            )
            return carry

        lax.fori_loop(begin, end, body, 0)

    def second_tiles(slot, count, begin, end):
        size = count * 4 * cap

        def body(i, carry):
            cols = columns(i, TILE)
            part[pl.ds(slot * 4 * cap, size), cols] = jnp.dot(
                hidden[pl.ds(0, size), :],
                w2[:, cols],
                preferred_element_type=jnp.float32,
            ).astype(jnp.bfloat16)
            return carry

        lax.fori_loop(begin, end, body, 0)

    n1, n2 = w1.shape[1] // TILE, w2.shape[1] // TILE

    def piece(slot, count, c):
        if c < 2:
            first_tiles(slot, count, c * n1 // 2, (c + 1) * n1 // 2)
        else:
            second_tiles(slot, count, (c - 2) * n2 // 2, (c - 1) * n2 // 2)

    own.wait()
    for c in range(4):
        if c:
            dispatch[c].wait_recv()
        forward(0, 0, c)
        forward(1, 0, c)
    loads[0].wait()
    loads[1].wait()
    for s in (1, 2, 3):
        for c in range(4):
            for way in (0, 1):
                arrivals[way, s, c].wait_recv()
                if s < 3 or c // 2 == way:
                    forward(way, s, c)
            if s == 1:
                piece(0, 1, c)
            else:
                piece(2 * s - 3, 2, c)
    for c in range(4):
        piece(5, 2, c)

    def rs_slot(way, t):
        return (7, 6 - way, 4 - way, 2 - way)[t]

    def rs_chunk(way, t, c):
        place = way * 14 + (c % 2 if t == 0 else 4 * t - 2 + c)
        return pl.ds(place * cap, cap)

    sums = {}

    def pass_on(way, t, c):
        sums[way, t, c] = send(
            part.at[chunk(rs_slot(way, t), c)],
            rs.at[rs_chunk(way, t, c)],
            r_send.at[way, t, c],
            r_recv.at[way, t, c],
            right if way == 0 else left,
        )

    def add_in(way, t, c):
        sums[way, t, c].wait_recv()
        here = chunk(rs_slot(way, t + 1), c)
        part[here, :] = (
            part[here, :].astype(jnp.float32)
            + rs[rs_chunk(way, t, c), :].astype(jnp.float32)
        ).astype(jnp.bfloat16)

    for c in (2, 3):
        pass_on(0, 1, c)
        pass_on(1, 1, c - 2)
    for c in (0, 1):
        arrivals[0, 4, c].wait_recv()
        arrivals[1, 4, c + 2].wait_recv()
    for c in range(4):
        piece(7, 1, c)
    for c in (0, 1):
        pass_on(0, 0, c)
        pass_on(1, 0, c + 2)
    for c in (0, 1):
        add_in(0, 0, c)
        pass_on(0, 1, c)
        add_in(1, 0, c + 2)
        pass_on(1, 1, c + 2)
    order = (2, 3, 0, 1)
    for t in (1, 2):
        for c in order:
            for way in (0, 1):
                add_in(way, t, c)
                pass_on(way, t + 1, c)

    returned = [None] * 4
    for c in order:
        sums[0, 3, c].wait_recv()
        sums[1, 3, c].wait_recv()
        here = chunk(0, c)
        total = (
            part[here, :].astype(jnp.float32)
            + rs[rs_chunk(0, 3, c), :].astype(jnp.float32)
            + rs[rs_chunk(1, 3, c), :].astype(jnp.float32)
        ).astype(jnp.bfloat16)
        if c == 0:
            ret[pl.ds(0, cap), :] = total
        else:
            part[here, :] = total
            returned[c] = send(
                part.at[here],
                ret.at[pl.ds(c * cap, cap)],
                ret_send.at[c],
                ret_recv.at[c],
                peers[c],
            )
    for c in (1, 2, 3):
        returned[c].wait_recv()

    tokens = residual.shape[0]
    half = tokens // 2

    def block(r, h=None):
        if h is None:
            return pl.ds(r * tokens, tokens)
        return pl.ds(r * tokens + h * half, half)

    from_sibling, from_y, from_far = [], [], []
    for h in range(2):
        some = pl.ds(h * half, half)
        group_out = jnp.dot(
            back_map[some, :], ret[...], preferred_element_type=jnp.float32
        )
        value = residual[some, :] + group_out
        middle[some, :] = value
        sgather[some, :] = layer_norm(value, gain2[...]).astype(jnp.bfloat16)
        from_y.append(
            send(
                sgather.at[some],
                sgather.at[block(2, h)],
                sg_send.at[0, h],
                sg_recv.at[0, h],
                peers[2],
            )
        )
        from_sibling.append(
            send(
                sgather.at[some],
                sgather.at[block(1, h)],
                sg_send.at[1, h],
                sg_recv.at[1, h],
                peers[1],
            )
        )

    m1, m2 = sw1.shape[1] // TILE, sw2.shape[1] // TILE

    def shared_first(pair):
        def body(i, carry):
            cols = columns(i, TILE)
            value = jnp.dot(
                sgather[pl.ds(pair * 2 * tokens, 2 * tokens), :],
                sw1[:, cols],
                preferred_element_type=jnp.float32,
            )
            shidden[:, cols] = jnp.maximum(value + sb1[:, cols], 0.0).astype(jnp.bfloat16)
            return carry

        lax.fori_loop(0, m1, body, 0)

    def shared_second(pair, begin, end):
        def body(i, carry):
            cols = columns(i, TILE)
            spart[pl.ds(pair * 2 * tokens, 2 * tokens), cols] = jnp.dot(
                shidden[...], sw2[:, cols], preferred_element_type=jnp.float32
            ).astype(jnp.bfloat16)
            return carry

        lax.fori_loop(begin, end, body, 0)

    loads[2].wait()
    loads[3].wait()
    for h in range(2):
        from_sibling[h].wait_recv()
    shared_first(0)
    for h in range(2):
        from_y[h].wait_recv()
        from_far.append(
            send(
                sgather.at[block(2, h)],
                sgather.at[block(3, h)],
                sg_send.at[2, h],
                sg_recv.at[2, h],
                peers[1],
            )
        )
    shared_second(0, 0, m2)
    to_own = send(
        spart.at[block(1)], sown, sr_send.at[2, 0], sr_recv.at[2, 0], peers[1]
    )
    for h in range(2):
        from_far[h].wait_recv()
    shared_first(1)
    quarters = 4
    width = sw2.shape[1] // quarters
    crossed, summed = [], []

    def finish_quarter(q):
        cols = pl.ds(q * width, width)
        crossed[q].wait_recv()
        spart[block(2), cols] = (
            spart[block(2), cols].astype(jnp.float32) + scross[:, cols].astype(jnp.float32)
        ).astype(jnp.bfloat16)
        summed.append(
            send(
                spart.at[block(2), cols],
                ssum.at[:, cols],
                sr_send.at[1, q],
                sr_recv.at[1, q],
                peers[2],
            )
        )

    for q in range(quarters):
        cols = pl.ds(q * width, width)
        shared_second(1, q * m2 // quarters, (q + 1) * m2 // quarters)
        crossed.append(
            send(
                spart.at[block(3), cols],
                scross.at[:, cols],
                sr_send.at[0, q],
                sr_recv.at[0, q],
                peers[1],
            )
        )
        if q:
            finish_quarter(q - 1)
    finish_quarter(quarters - 1)
    to_own.wait_recv()
    for q in range(quarters):
        cols = pl.ds(q * width, width)
        summed[q].wait_recv()
        encoded[:, cols] = (
            middle[:, cols]
            + (
                spart[block(0), cols].astype(jnp.float32)
                + sown[:, cols].astype(jnp.float32)
                + ssum[:, cols].astype(jnp.float32)
            )
            + sb2[:, cols]
        ).astype(jnp.bfloat16)
    for copy in pending:
        copy.wait_send()


def fused_on_device(
    tokens,
    languages,
    lang_group,
    group_gain,
    group_w1,
    group_b1,
    group_w2,
    group_b2,
    shared_gain,
    shared_w1,
    shared_b1,
    shared_w2,
    shared_b2,
):
    tok_dev, width = tokens.shape
    num_groups = group_gain.shape[0]
    num_langs = lang_group.shape[0]
    cap = 3 * tok_dev // (2 * num_groups)
    me = lax.axis_index("group")
    residual = tokens.astype(jnp.float32)
    lang_hit = languages[:, None] == jnp.arange(num_langs, dtype=jnp.int32)[None, :]
    group_of = jnp.sum(jnp.where(lang_hit, lang_group[None, :], 0), axis=1)
    onehot = group_of[:, None] == jnp.arange(num_groups, dtype=jnp.int32)[None, :]
    same = group_of[:, None] == group_of[None, :]
    index = jnp.arange(tok_dev, dtype=jnp.int32)
    before = index[None, :] < index[:, None]
    slot_index = jnp.sum((same & before).astype(jnp.int32), axis=1)
    position = (group_of ^ me) * cap + slot_index
    slots = jnp.arange(num_groups * cap, dtype=jnp.int32)
    out_map = (position[None, :] == slots[:, None]).astype(jnp.bfloat16)
    back_map = (position[:, None] == slots[None, :]).astype(jnp.bfloat16)
    onehot_float = onehot.astype(jnp.float32)
    row_gains = jnp.dot(onehot_float, group_gain, precision=lax.Precision.HIGHEST)
    normed = layer_norm(residual, row_gains).astype(jnp.bfloat16)
    outgoing = jnp.dot(out_map, normed, preferred_element_type=jnp.float32).astype(
        jnp.bfloat16
    )
    group_bias = jnp.dot(onehot_float, group_b2, precision=lax.Precision.HIGHEST)
    unit = group_w1.shape[2]
    shared_unit = shared_w1.shape[1]
    rows = num_groups * cap
    bf16, f32 = jnp.bfloat16, jnp.float32
    in_vmem = pl.BlockSpec(memory_space=pltpu.VMEM)
    anywhere = pl.BlockSpec(memory_space=pl.ANY)
    dma = pltpu.SemaphoreType.DMA
    return pl.pallas_call(
        functools.partial(fused_kernel, cap),
        out_shape=jax.ShapeDtypeStruct((tok_dev, width), bf16),
        in_specs=[in_vmem] * 7 + [anywhere] * 4,
        out_specs=in_vmem,
        scratch_shapes=[
            pltpu.VMEM((width, unit), bf16),
            pltpu.VMEM((unit, width), bf16),
            pltpu.VMEM((width, shared_unit), bf16),
            pltpu.VMEM((shared_unit, width), bf16),
            pltpu.VMEM((8 * rows, width), bf16),
            pltpu.VMEM((8 * rows, width), bf16),
            pltpu.VMEM((7 * rows, width), bf16),
            pltpu.VMEM((2 * rows, unit), bf16),
            pltpu.VMEM((rows, width), bf16),
            pltpu.VMEM((4 * tok_dev, width), bf16),
            pltpu.VMEM((2 * tok_dev, shared_unit), bf16),
            pltpu.VMEM((4 * tok_dev, width), bf16),
            pltpu.VMEM((tok_dev, width), bf16),
            pltpu.VMEM((tok_dev, width), bf16),
            pltpu.VMEM((tok_dev, width), bf16),
            pltpu.VMEM((tok_dev, width), f32),
            dma((4,)),
            dma,
            dma((4,)),
            dma((4,)),
            dma((2, 4, 4)),
            dma((2, 5, 4)),
            dma((2, 4, 4)),
            dma((2, 4, 4)),
            dma((4,)),
            dma((4,)),
            dma((3, 2)),
            dma((3, 2)),
            dma((3, 4)),
            dma((3, 4)),
        ],
        compiler_params=pltpu.CompilerParams(
            collective_id=0, has_side_effects=True, vmem_limit_bytes=62 * 1024 * 1024
        ),
    )(
        outgoing,
        back_map,
        residual + group_bias,
        group_b1,
        shared_gain[None, :],
        shared_b1[None, :],
        shared_b2[None, :],
        group_w1[0],
        group_w2[0],
        shared_w1,
        shared_w2,
    )


def plain_on_device(
    tokens,
    languages,
    lang_group,
    group_gain,
    group_w1,
    group_b1,
    group_w2,
    group_b2,
    shared_gain,
    shared_w1,
    shared_b1,
    shared_w2,
    shared_b2,
):
    tok_dev = tokens.shape[0]
    width_model = tokens.shape[1]
    num_groups = group_gain.shape[0]
    num_langs = lang_group.shape[0]
    capacity = 3 * tok_dev // (2 * lax.axis_size("group"))
    residual_in = tokens.astype(jnp.float32)
    lang_hit = (languages[:, None] == jnp.arange(num_langs, dtype=jnp.int32)[None, :]).astype(
        jnp.int32
    )
    group_of = jnp.sum(lang_hit * lang_group[None, :], axis=1)
    onehot = (group_of[:, None] == jnp.arange(num_groups, dtype=jnp.int32)[None, :]).astype(
        jnp.int32
    )
    earlier = jnp.cumsum(onehot, axis=0) - onehot
    slot_index = jnp.sum(earlier * onehot, axis=1)
    position = group_of * capacity + slot_index
    dispatch_map = (
        position[None, :] == jnp.arange(num_groups * capacity, dtype=jnp.int32)[:, None]
    ).astype(jnp.bfloat16)
    onehot_float = onehot.astype(jnp.float32)
    row_gains = jnp.dot(onehot_float, group_gain, precision=lax.Precision.HIGHEST)
    normed = layer_norm(residual_in, row_gains).astype(jnp.bfloat16)
    outgoing = jnp.dot(dispatch_map, normed, preferred_element_type=jnp.float32).astype(
        jnp.bfloat16
    )
    outgoing = outgoing.reshape(num_groups, capacity, width_model)
    arrived = lax.all_to_all(outgoing, "group", split_axis=0, concat_axis=0, tiled=True)
    group_rows = arrived.reshape(num_groups * capacity, width_model)
    first_proj = group_w1[0]
    first_bias = group_b1[0]
    second_proj = group_w2[0]
    hidden = jax.nn.relu(
        jnp.dot(
            lax.all_gather(group_rows, "within", axis=0, tiled=True),
            first_proj,
            preferred_element_type=jnp.float32,
        )
        + first_bias
    ).astype(jnp.bfloat16)
    selected = hidden
    summed = lax.psum_scatter(
        jnp.dot(selected, second_proj, preferred_element_type=jnp.float32).astype(jnp.bfloat16),
        "within",
        scatter_dimension=0,
        tiled=True,
    )
    returned = lax.all_to_all(
        summed.reshape(num_groups, capacity, width_model),
        "group",
        split_axis=0,
        concat_axis=0,
        tiled=True,
    )
    returned = returned.reshape(num_groups * capacity, width_model)
    group_out = lax.dot_general(
        dispatch_map, returned, (((0,), (0,)), ((), ())), preferred_element_type=jnp.float32
    )
    group_bias = jnp.dot(onehot_float, group_b2, precision=lax.Precision.HIGHEST)
    middle = residual_in + group_out + group_bias
    shared_in = layer_norm(middle, shared_gain).astype(jnp.bfloat16)
    shared_hidden = jax.nn.relu(
        jnp.dot(
            lax.all_gather(shared_in, "group", axis=0, tiled=True),
            shared_w1,
            preferred_element_type=jnp.float32,
        )
        + shared_b1
    ).astype(jnp.bfloat16)
    selected = shared_hidden
    shared_out = lax.psum_scatter(
        jnp.dot(selected, shared_w2, preferred_element_type=jnp.float32).astype(jnp.bfloat16),
        "group",
        scatter_dimension=0,
        tiled=True,
    ).astype(jnp.float32)
    return (middle + shared_out + shared_b2).astype(jnp.bfloat16)


def solution(mesh):
    placed = (
        P(("group", "within"), None),
        P(("group", "within")),
        P(),
        P(),
        P("group", None, "within"),
        P("group", "within"),
        P("group", "within", None),
        P(),
        P(),
        P(None, "group"),
        P("group"),
        P("group", None),
        P(),
    )
    fits = mesh.shape["group"] == 4 and mesh.shape["within"] == 8
    return jax.shard_map(
        fused_on_device if fits else plain_on_device,
        mesh=mesh,
        in_specs=placed,
        out_specs=P(("group", "within"), None),
        check_vma=False,
    )
```

```python
import jax
import jax.numpy as jnp
from jax import lax
from jax.experimental import pallas as pl
from jax.experimental.pallas import tpu as pltpu
from jax.sharding import PartitionSpec as P

MESH = pl.DeviceIdType.MESH
TILE = 256


def layer_norm(values, gains):
    centre = jnp.mean(values, axis=-1, keepdims=True)
    centred = values - centre
    spread = jnp.mean(centred * centred, axis=-1, keepdims=True)
    return centred * lax.rsqrt(spread + 1e-05) * gains


def columns(tile, size):
    return pl.ds(pl.multiple_of(tile * size, size), size)


def row_sum(mask):
    return jnp.sum(jnp.where(mask, 1.0, 0.0), axis=1, keepdims=True)


def column_sum(mask):
    return jnp.sum(jnp.where(mask, 1.0, 0.0), axis=0, keepdims=True)


def by_group(column, table):
    value = jnp.where(column == 0.0, table[0:1, :], 0.0)
    for i in range(1, table.shape[0]):
        value = jnp.where(column == float(i), table[i : i + 1, :], value)
    return value


def fused_kernel(
    tokens,
    languages,
    lang_group,
    group_gain,
    group_b2,
    b1,
    gain2,
    sb1,
    sb2,
    w1_hbm,
    w2_hbm,
    sw1_hbm,
    sw2_hbm,
    encoded,
    w1,
    w2,
    sw1,
    sw2,
    outgoing,
    rows_a,
    part_a,
    rs_a,
    ret_a,
    rows_b,
    part_b,
    rs_b,
    ret_b,
    hidden,
    sgather,
    shidden,
    spart,
    sown,
    scross,
    ssum,
    middle,
    sgather_b,
    shidden_b,
    spart_b,
    sown_b,
    scross_b,
    ssum_b,
    middle_b,
    back_a,
    back_b,
    compact,
    spread,
    w_sem,
    local_sem,
    disp_send,
    disp_recv,
    g_send,
    g_recv,
    r_send,
    r_recv,
    ret_send,
    ret_recv,
    sg_send,
    sg_recv,
    sr_send,
    sr_recv,
):
    bf16, f32 = jnp.bfloat16, jnp.float32
    g = lax.axis_index("group")
    w = lax.axis_index("within")
    x, z = lax.rem(w, 2), lax.div(w, 2)
    p = z + x * (7 - 2 * z)

    def device_at(q):
        q = lax.rem(q + 8, 8)
        far = lax.div(q, 4)
        return 2 * q + far * (15 - 4 * q)

    right = (g, device_at(p + 1))
    left = (g, device_at(p - 1))
    yy, core = lax.div(g, 2), lax.rem(g, 2)
    peers = [
        None,
        (2 * yy + 1 - core, w),
        (2 * (1 - yy) + core, w),
        (2 * (1 - yy) + 1 - core, w),
    ]
    barrier = pltpu.get_barrier_semaphore()
    for device in (right, left, peers[1], peers[2], peers[3]):
        pl.semaphore_signal(barrier, inc=1, device_id=device, device_id_type=MESH)

    loads = []
    for i, (src, dst) in enumerate(
        ((w1_hbm, w1), (w2_hbm, w2), (sw1_hbm, sw1), (sw2_hbm, sw2))
    ):
        copy = pltpu.make_async_copy(src, dst, w_sem.at[i])
        copy.start()
        loads.append(copy)

    count = tokens.shape[0]
    cap_a, cap_b = count // 4, count // 8
    late = count // 4
    i0 = lax.broadcasted_iota(jnp.int32, (count, count), 0)
    i1 = lax.broadcasted_iota(jnp.int32, (count, count), 1)
    eye = i0 == i1

    def to_column(row):
        return jnp.sum(jnp.where(eye, row, 0.0), axis=1, keepdims=True)

    def to_row(column):
        return jnp.sum(jnp.where(eye, column, 0.0), axis=0, keepdims=True)

    num_langs = lang_group.shape[1]
    lang = to_column(languages[...].astype(f32))
    lang_ids = lax.broadcasted_iota(jnp.int32, (count, num_langs), 1).astype(f32)
    group_column = jnp.sum(
        jnp.where(lang == lang_ids, lang_group[...].astype(f32), 0.0), axis=1, keepdims=True
    )
    group_row = to_row(group_column)
    same = group_column == group_row
    slot_column = row_sum(same & (i1 < i0))
    slot_row = column_sum(same & (i0 < i1))
    my_y, my_core = yy.astype(f32), core.astype(f32)

    def position(group, slot):
        gy = jnp.where(group >= 2.0, 1.0, 0.0)
        dy, dc = gy - my_y, group - 2.0 * gy - my_core
        r = 2.0 * dy * dy + dc * dc
        return jnp.where(
            slot < cap_a, r * cap_a + slot, count + r * cap_b + slot - cap_a
        )

    place_column = position(group_column, slot_column)
    place_row = position(group_row, slot_row)
    total_slots = 4 * (cap_a + cap_b)
    out_map = (
        lax.broadcasted_iota(jnp.int32, (total_slots, count), 0).astype(f32) == place_row
    )
    normed = layer_norm(
        tokens[...].astype(f32), by_group(group_column, group_gain)
    ).astype(bf16)
    outgoing[...] = jnp.dot(
        jnp.where(out_map, 1.0, 0.0).astype(bf16), normed, preferred_element_type=f32
    ).astype(bf16)
    base = {"a": 0, "b": 4 * cap_a}
    caps = {"a": cap_a, "b": cap_b}
    stage = {"a": 0, "b": 1}
    rows = {"a": rows_a, "b": rows_b}
    part = {"a": part_a, "b": part_b}
    rs = {"a": rs_a, "b": rs_b}
    ret = {"a": ret_a, "b": ret_b}
    own = {}
    for k in "ab":
        own[k] = pltpu.make_async_copy(
            outgoing.at[pl.ds(base[k], caps[k])],
            rows[k].at[pl.ds(0, caps[k])],
            local_sem.at[stage[k]],
        )
        own[k].start()
    pl.semaphore_wait(barrier, 5)

    pending = []

    def send(src, dst, send_sem, recv_sem, device):
        copy = pltpu.make_async_remote_copy(
            src_ref=src,
            dst_ref=dst,
            send_sem=send_sem,
            recv_sem=recv_sem,
            device_id=device,
            device_id_type=MESH,
        )
        copy.start()
        pending.append(copy)
        return copy

    def chunk(k, slot, c):
        return pl.ds((slot * 4 + c) * caps[k], caps[k])

    dispatch = {}
    for k in "ab":
        for r in (2, 3, 1):
            dispatch[k, r] = send(
                outgoing.at[pl.ds(base[k] + r * caps[k], caps[k])],
                rows[k].at[chunk(k, 0, r)],
                disp_send.at[stage[k], r],
                disp_recv.at[stage[k], r],
                peers[r],
            )

    def slot_of(way, s):
        return 7 if s == 4 else (0 if s == 0 else 2 * s - 1 + way)

    arrivals = {}

    def forward(k, way, s, c):
        arrivals[k, way, s + 1, c] = send(
            rows[k].at[chunk(k, slot_of(way, s), c)],
            rows[k].at[chunk(k, slot_of(way, s + 1), c)],
            g_send.at[stage[k], way, s, c],
            g_recv.at[stage[k], way, s + 1, c],
            right if way == 0 else left,
        )

    def first_tiles(k, slot, slots, begin, end):
        size = slots * 4 * caps[k]

        def body(i, carry):
            cols = columns(i, TILE)
            value = jnp.dot(
                rows[k][pl.ds(slot * 4 * caps[k], size), :],
                w1[:, cols],
                preferred_element_type=f32,
            )
            hidden[pl.ds(0, size), cols] = jnp.maximum(value + b1[:, cols], 0.0).astype(bf16)
            return carry

        lax.fori_loop(begin, end, body, 0)

    def second_tiles(k, slot, slots, begin, end):
        size = slots * 4 * caps[k]

        def body(i, carry):
            cols = columns(i, TILE)
            part[k][pl.ds(slot * 4 * caps[k], size), cols] = jnp.dot(
                hidden[pl.ds(0, size), :], w2[:, cols], preferred_element_type=f32
            ).astype(bf16)
            return carry

        lax.fori_loop(begin, end, body, 0)

    n1, n2 = w1.shape[1] // TILE, w2.shape[1] // TILE

    def piece(k, slot, slots, c):
        if c < 2:
            first_tiles(k, slot, slots, c * n1 // 2, (c + 1) * n1 // 2)
        else:
            second_tiles(k, slot, slots, (c - 2) * n2 // 2, (c - 1) * n2 // 2)

    def whole(k, slot, slots):
        first_tiles(k, slot, slots, 0, n1)
        second_tiles(k, slot, slots, 0, n2)

    def gather_start(k):
        own[k].wait()
        for c in range(4):
            if c:
                dispatch[k, c].wait_recv()
            forward(k, 0, 0, c)
            forward(k, 1, 0, c)

    def gather_step(k, s, c):
        for way in (0, 1):
            arrivals[k, way, s, c].wait_recv()
            if s < 3 or c // 2 == way:
                forward(k, way, s, c)

    def rs_slot(way, t):
        return (7, 6 - way, 4 - way, 2 - way)[t]

    def rs_chunk(k, way, t, c):
        at = way * 14 + (c % 2 if t == 0 else 4 * t - 2 + c)
        return pl.ds(at * caps[k], caps[k])

    sums = {}

    def pass_on(k, way, t, c):
        sums[k, way, t, c] = send(
            part[k].at[chunk(k, rs_slot(way, t), c)],
            rs[k].at[rs_chunk(k, way, t, c)],
            r_send.at[stage[k], way, t, c],
            r_recv.at[stage[k], way, t, c],
            right if way == 0 else left,
        )

    def add_in(k, way, t, c):
        sums[k, way, t, c].wait_recv()
        here = chunk(k, rs_slot(way, t + 1), c)
        part[k][here, :] = (
            part[k][here, :].astype(f32) + rs[k][rs_chunk(k, way, t, c), :].astype(f32)
        ).astype(bf16)
        pass_on(k, way, t + 1, c)

    order = (2, 3, 0, 1)

    def reduce_start(k, between):
        for c in (2, 3):
            pass_on(k, 0, 1, c)
            pass_on(k, 1, 1, c - 2)
        between()
        for c in (0, 1):
            arrivals[k, 0, 4, c].wait_recv()
            arrivals[k, 1, 4, c + 2].wait_recv()
        whole(k, 7, 1)
        for c in (0, 1):
            pass_on(k, 0, 0, c)
            pass_on(k, 1, 0, c + 2)
        between()
        for c in (0, 1):
            add_in(k, 0, 0, c)
            add_in(k, 1, 0, c + 2)

    returned = {}

    def reduce_end(k, c):
        sums[k, 0, 3, c].wait_recv()
        sums[k, 1, 3, c].wait_recv()
        here = chunk(k, 0, c)
        total = (
            part[k][here, :].astype(f32)
            + rs[k][rs_chunk(k, 0, 3, c), :].astype(f32)
            + rs[k][rs_chunk(k, 1, 3, c), :].astype(f32)
        ).astype(bf16)
        if c == 0:
            ret[k][pl.ds(0, caps[k]), :] = total
        else:
            part[k][here, :] = total
            returned[k, c] = send(
                part[k].at[here],
                ret[k].at[pl.ds(c * caps[k], caps[k])],
                ret_send.at[stage[k], c],
                ret_recv.at[stage[k], c],
                peers[c],
            )

    m1, m2 = sw1.shape[1] // TILE, sw2.shape[1] // TILE

    def shared_first(source, start, size, target, begin, end):
        def body(i, carry):
            cols = columns(i, TILE)
            value = jnp.dot(
                source[pl.ds(start, size), :], sw1[:, cols], preferred_element_type=f32
            )
            target[:, cols] = jnp.maximum(value + sb1[:, cols], 0.0).astype(bf16)
            return carry

        lax.fori_loop(begin, end, body, 0)

    def shared_second(source, target, start, size, begin, end):
        def body(i, carry):
            cols = columns(i, TILE)
            target[pl.ds(start, size), cols] = jnp.dot(
                source[...], sw2[:, cols], preferred_element_type=f32
            ).astype(bf16)
            return carry

        lax.fori_loop(begin, end, body, 0)

    quarters = 4
    width = sw2.shape[1] // quarters

    def quarter(q):
        return pl.ds(q * width, width)

    def add_crossed(source, cross, target, at, copy, send_sem, recv_sem, q):
        cols = quarter(q)
        copy.wait_recv()
        source[at, cols] = (
            source[at, cols].astype(f32) + cross[:, cols].astype(f32)
        ).astype(bf16)
        return send(source.at[at, cols], target.at[:, cols], send_sem, recv_sem, peers[2])

    def combined(total, own_part, sibling, crossed, cols):
        return (
            total
            + (own_part.astype(f32) + sibling.astype(f32) + crossed.astype(f32))
            + sb2[:, cols]
        )

    half = count // 2

    def block(r, h=None):
        if h is None:
            return pl.ds(r * count, count)
        return pl.ds(r * count + h * half, half)

    def shared_a():
        for c in (1, 2, 3):
            returned["a", c].wait_recv()
        from_sibling, from_y, from_far = [], [], []
        for h in range(2):
            some = pl.ds(h * half, half)
            value = middle[some, :] + jnp.dot(
                back_a[some, :], ret_a[...], preferred_element_type=f32
            )
            middle[some, :] = value
            sgather[some, :] = layer_norm(value, gain2[...]).astype(bf16)
            for r, into in ((2, from_y), (1, from_sibling)):
                into.append(
                    send(
                        sgather.at[some],
                        sgather.at[block(r, h)],
                        sg_send.at[r, h],
                        sg_recv.at[r, h],
                        peers[r],
                    )
                )
        yield
        loads[2].wait()
        loads[3].wait()
        for h in range(2):
            from_sibling[h].wait_recv()
        for q in range(4):
            shared_first(sgather, 0, 2 * count, shidden, q * m1 // 4, (q + 1) * m1 // 4)
            yield
        for q in range(4):
            shared_second(shidden, spart, 0, 2 * count, q * m2 // 4, (q + 1) * m2 // 4)
            yield
        to_own = send(
            spart.at[block(1)], sown, sr_send.at[2, 0], sr_recv.at[2, 0], peers[1]
        )
        yield
        for h in range(2):
            from_y[h].wait_recv()
            from_far.append(
                send(
                    sgather.at[block(2, h)],
                    sgather.at[block(3, h)],
                    sg_send.at[3, h],
                    sg_recv.at[3, h],
                    peers[1],
                )
            )
            yield
        for h in range(2):
            from_far[h].wait_recv()
        for q in range(4):
            shared_first(
                sgather, 2 * count, 2 * count, shidden, q * m1 // 4, (q + 1) * m1 // 4
            )
            yield
        crossed, summed = [], []

        def finish(q):
            summed.append(
                add_crossed(
                    spart, scross, ssum, block(2), crossed[q], sr_send.at[1, q], sr_recv.at[1, q], q
                )
            )

        for q in range(quarters):
            shared_second(
                shidden, spart, 2 * count, 2 * count, q * m2 // 4, (q + 1) * m2 // 4
            )
            crossed.append(
                send(
                    spart.at[block(3), quarter(q)],
                    scross.at[:, quarter(q)],
                    sr_send.at[0, q],
                    sr_recv.at[0, q],
                    peers[1],
                )
            )
            if q:
                finish(q - 1)
            yield
        finish(quarters - 1)
        yield
        to_own.wait_recv()
        for q in range(quarters):
            cols = quarter(q)
            summed[q].wait_recv()
            middle[:, cols] = combined(
                middle[:, cols], spart[block(0), cols], sown[:, cols], ssum[:, cols], cols
            )
            yield

    gather_start("a")
    back_a[...] = jnp.where(
        lax.broadcasted_iota(jnp.int32, (count, 4 * cap_a), 1).astype(f32) == place_column,
        1.0,
        0.0,
    ).astype(bf16)
    middle[...] = tokens[...].astype(f32) + by_group(group_column, group_b2)
    rank_row = column_sum((slot_column >= cap_a) & (i0 < i1))
    rank_row = jnp.where(slot_row >= cap_a, rank_row, -1.0)
    rank_column = row_sum((slot_row >= cap_a) & (i1 < i0))
    rank_column = jnp.where(slot_column >= cap_a, rank_column, -1.0)
    pick = jnp.where(
        lax.broadcasted_iota(jnp.int32, (late, count), 0).astype(f32) == rank_row, 1.0, 0.0
    )
    compact[...] = pick.astype(bf16)
    spread[...] = jnp.where(
        lax.broadcasted_iota(jnp.int32, (count, late), 1).astype(f32) == rank_column, 1.0, 0.0
    ).astype(bf16)
    late_place = jnp.sum(pick * place_row, axis=1, keepdims=True) - 4.0 * cap_a
    late_group = jnp.sum(pick * group_row, axis=1, keepdims=True)
    back_b[...] = jnp.where(
        lax.broadcasted_iota(jnp.int32, (late, 4 * cap_b), 1).astype(f32) == late_place,
        1.0,
        0.0,
    ).astype(bf16)
    middle_b[...] = jnp.dot(
        compact[...], tokens[...], preferred_element_type=f32
    ) + by_group(late_group, group_b2)
    loads[0].wait()
    loads[1].wait()
    for s in (1, 2, 3):
        for c in range(4):
            gather_step("a", s, c)
            if s == 1:
                piece("a", 0, 1, c)
            else:
                piece("a", 2 * s - 3, 2, c)
    whole("a", 5, 2)
    reduce_start("a", lambda: None)
    for t in (1, 2):
        for c in order:
            for way in (0, 1):
                add_in("a", way, t, c)

    gather_start("b")
    for c in order:
        reduce_end("a", c)
    shared = shared_a()

    def go_on():
        next(shared, None)

    for s in (1, 2, 3):
        for c in range(4):
            gather_step("b", s, c)
            if s == 3:
                piece("b", 0, 5, c)
            go_on()
    whole("b", 5, 2)
    reduce_start("b", go_on)
    for t in (1, 2):
        for c in order:
            for way in (0, 1):
                add_in("b", way, t, c)
            go_on()
    for c in order:
        reduce_end("b", c)
        go_on()
    for _ in shared:
        pass

    for c in (1, 2, 3):
        returned["b", c].wait_recv()

    def block_b(r):
        return pl.ds(r * late, late)

    value = middle_b[...] + jnp.dot(back_b[...], ret_b[...], preferred_element_type=f32)
    middle_b[...] = value
    sgather_b[block_b(0), :] = layer_norm(value, gain2[...]).astype(bf16)
    near = {}
    for r in (2, 1):
        near[r] = send(
            sgather_b.at[block_b(0)],
            sgather_b.at[block_b(r)],
            sg_send.at[r, 2],
            sg_recv.at[r, 2],
            peers[r],
        )
    near[2].wait_recv()
    near[3] = send(
        sgather_b.at[block_b(2)],
        sgather_b.at[block_b(3)],
        sg_send.at[3, 2],
        sg_recv.at[3, 2],
        peers[1],
    )
    near[1].wait_recv()
    near[3].wait_recv()
    shared_first(sgather_b, 0, 4 * late, shidden_b, 0, m1)
    crossed, to_own, summed = [], [], []

    def finish_b(q):
        summed.append(
            add_crossed(
                spart_b,
                scross_b,
                ssum_b,
                block_b(2),
                crossed[q],
                sr_send.at[4, q],
                sr_recv.at[4, q],
                q,
            )
        )

    for q in range(quarters):
        cols = quarter(q)
        shared_second(shidden_b, spart_b, 0, 4 * late, q * m2 // 4, (q + 1) * m2 // 4)
        crossed.append(
            send(
                spart_b.at[block_b(3), cols],
                scross_b.at[:, cols],
                sr_send.at[3, q],
                sr_recv.at[3, q],
                peers[1],
            )
        )
        to_own.append(
            send(
                spart_b.at[block_b(1), cols],
                sown_b.at[:, cols],
                sr_send.at[5, q],
                sr_recv.at[5, q],
                peers[1],
            )
        )
        if q:
            finish_b(q - 1)
    finish_b(quarters - 1)
    for q in range(quarters):
        cols = quarter(q)
        to_own[q].wait_recv()
        summed[q].wait_recv()
        late_out = combined(
            middle_b[:, cols], spart_b[block_b(0), cols], sown_b[:, cols], ssum_b[:, cols], cols
        ).astype(bf16)
        placed = jnp.dot(spread[...], late_out, preferred_element_type=f32)
        is_late = jnp.sum(spread[...].astype(f32), axis=1, keepdims=True)
        encoded[:, cols] = jnp.where(is_late > 0.5, placed, middle[:, cols]).astype(bf16)
    for copy in pending:
        copy.wait_send()


def fused_on_device(
    tokens,
    languages,
    lang_group,
    group_gain,
    group_w1,
    group_b1,
    group_w2,
    group_b2,
    shared_gain,
    shared_w1,
    shared_b1,
    shared_w2,
    shared_b2,
):
    count, width = tokens.shape
    unit = group_w1.shape[2]
    shared_unit = shared_w1.shape[1]
    cap_a, cap_b = count // 4, count // 8
    late = count // 4
    bf16, f32 = jnp.bfloat16, jnp.float32
    in_vmem = pl.BlockSpec(memory_space=pltpu.VMEM)
    anywhere = pl.BlockSpec(memory_space=pl.ANY)
    dma = pltpu.SemaphoreType.DMA

    def held(rows, columns=width, dtype=bf16):
        return pltpu.VMEM((rows, columns), dtype)

    return pl.pallas_call(
        fused_kernel,
        out_shape=jax.ShapeDtypeStruct((count, width), bf16),
        in_specs=[in_vmem] * 9 + [anywhere] * 4,
        out_specs=in_vmem,
        scratch_shapes=[
            held(width, unit),
            held(unit),
            held(width, shared_unit),
            held(shared_unit),
            held(4 * (cap_a + cap_b)),
            held(32 * cap_a),
            held(32 * cap_a),
            held(28 * cap_a),
            held(4 * cap_a),
            held(32 * cap_b),
            held(32 * cap_b),
            held(28 * cap_b),
            held(4 * cap_b),
            held(max(8 * cap_a, 20 * cap_b), unit),
            held(4 * count),
            held(2 * count, shared_unit),
            held(4 * count),
            held(count),
            held(count),
            held(count),
            held(count, dtype=f32),
            held(4 * late),
            held(4 * late, shared_unit),
            held(4 * late),
            held(late),
            held(late),
            held(late),
            held(late, dtype=f32),
            held(count, 4 * cap_a),
            held(late, 4 * cap_b),
            held(late, count),
            held(count, late),
            dma((4,)),
            dma((2,)),
            dma((2, 4)),
            dma((2, 4)),
            dma((2, 2, 4, 4)),
            dma((2, 2, 5, 4)),
            dma((2, 2, 4, 4)),
            dma((2, 2, 4, 4)),
            dma((2, 4)),
            dma((2, 4)),
            dma((4, 3)),
            dma((4, 3)),
            dma((6, 4)),
            dma((6, 4)),
        ],
        compiler_params=pltpu.CompilerParams(
            collective_id=0, has_side_effects=True, vmem_limit_bytes=62 * 1024 * 1024
        ),
    )(
        tokens,
        languages[None, :],
        lang_group[None, :],
        group_gain,
        group_b2,
        group_b1,
        shared_gain[None, :],
        shared_b1[None, :],
        shared_b2[None, :],
        group_w1[0],
        group_w2[0],
        shared_w1,
        shared_w2,
    )


def plain_on_device(
    tokens,
    languages,
    lang_group,
    group_gain,
    group_w1,
    group_b1,
    group_w2,
    group_b2,
    shared_gain,
    shared_w1,
    shared_b1,
    shared_w2,
    shared_b2,
):
    tok_dev = tokens.shape[0]
    width_model = tokens.shape[1]
    num_groups = group_gain.shape[0]
    num_langs = lang_group.shape[0]
    capacity = 3 * tok_dev // (2 * lax.axis_size("group"))
    residual_in = tokens.astype(jnp.float32)
    lang_hit = (languages[:, None] == jnp.arange(num_langs, dtype=jnp.int32)[None, :]).astype(
        jnp.int32
    )
    group_of = jnp.sum(lang_hit * lang_group[None, :], axis=1)
    onehot = (group_of[:, None] == jnp.arange(num_groups, dtype=jnp.int32)[None, :]).astype(
        jnp.int32
    )
    earlier = jnp.cumsum(onehot, axis=0) - onehot
    slot_index = jnp.sum(earlier * onehot, axis=1)
    position = group_of * capacity + slot_index
    dispatch_map = (
        position[None, :] == jnp.arange(num_groups * capacity, dtype=jnp.int32)[:, None]
    ).astype(jnp.bfloat16)
    onehot_float = onehot.astype(jnp.float32)
    row_gains = jnp.dot(onehot_float, group_gain, precision=lax.Precision.HIGHEST)
    normed = layer_norm(residual_in, row_gains).astype(jnp.bfloat16)
    outgoing = jnp.dot(dispatch_map, normed, preferred_element_type=jnp.float32).astype(
        jnp.bfloat16
    )
    outgoing = outgoing.reshape(num_groups, capacity, width_model)
    arrived = lax.all_to_all(outgoing, "group", split_axis=0, concat_axis=0, tiled=True)
    group_rows = arrived.reshape(num_groups * capacity, width_model)
    first_proj = group_w1[0]
    first_bias = group_b1[0]
    second_proj = group_w2[0]
    hidden = jax.nn.relu(
        jnp.dot(
            lax.all_gather(group_rows, "within", axis=0, tiled=True),
            first_proj,
            preferred_element_type=jnp.float32,
        )
        + first_bias
    ).astype(jnp.bfloat16)
    selected = hidden
    summed = lax.psum_scatter(
        jnp.dot(selected, second_proj, preferred_element_type=jnp.float32).astype(jnp.bfloat16),
        "within",
        scatter_dimension=0,
        tiled=True,
    )
    returned = lax.all_to_all(
        summed.reshape(num_groups, capacity, width_model),
        "group",
        split_axis=0,
        concat_axis=0,
        tiled=True,
    )
    returned = returned.reshape(num_groups * capacity, width_model)
    group_out = lax.dot_general(
        dispatch_map, returned, (((0,), (0,)), ((), ())), preferred_element_type=jnp.float32
    )
    group_bias = jnp.dot(onehot_float, group_b2, precision=lax.Precision.HIGHEST)
    middle = residual_in + group_out + group_bias
    shared_in = layer_norm(middle, shared_gain).astype(jnp.bfloat16)
    shared_hidden = jax.nn.relu(
        jnp.dot(
            lax.all_gather(shared_in, "group", axis=0, tiled=True),
            shared_w1,
            preferred_element_type=jnp.float32,
        )
        + shared_b1
    ).astype(jnp.bfloat16)
    selected = shared_hidden
    shared_out = lax.psum_scatter(
        jnp.dot(selected, shared_w2, preferred_element_type=jnp.float32).astype(jnp.bfloat16),
        "group",
        scatter_dimension=0,
        tiled=True,
    ).astype(jnp.float32)
    return (middle + shared_out + shared_b2).astype(jnp.bfloat16)


def solution(mesh):
    placed = (
        P(("group", "within"), None),
        P(("group", "within")),
        P(),
        P(),
        P("group", None, "within"),
        P("group", "within"),
        P("group", "within", None),
        P(),
        P(),
        P(None, "group"),
        P("group"),
        P("group", None),
        P(),
    )
    fits = mesh.shape["group"] == 4 and mesh.shape["within"] == 8
    return jax.shard_map(
        fused_on_device if fits else plain_on_device,
        mesh=mesh,
        in_specs=placed,
        out_specs=P(("group", "within"), None),
        check_vma=False,
    )
```

```python
import jax
import jax.numpy as jnp
from jax import lax
from jax.experimental import pallas as pl
from jax.experimental.pallas import tpu as pltpu
from jax.sharding import PartitionSpec as P

MESH = pl.DeviceIdType.MESH
TILE = 256


def layer_norm(values, gains):
    centre = jnp.mean(values, axis=-1, keepdims=True)
    centred = values - centre
    spread = jnp.mean(centred * centred, axis=-1, keepdims=True)
    return centred * lax.rsqrt(spread + 1e-05) * gains


def columns(tile, size):
    return pl.ds(pl.multiple_of(tile * size, size), size)


def row_sum(mask):
    return jnp.sum(jnp.where(mask, 1.0, 0.0), axis=1, keepdims=True)


def column_sum(mask):
    return jnp.sum(jnp.where(mask, 1.0, 0.0), axis=0, keepdims=True)


def by_group(column, table):
    value = jnp.where(column == 0.0, table[0:1, :], 0.0)
    for i in range(1, table.shape[0]):
        value = jnp.where(column == float(i), table[i : i + 1, :], value)
    return value


def fused_kernel(
    tokens,
    languages,
    lang_group,
    group_gain,
    group_b2,
    b1,
    gain2,
    sb1,
    sb2,
    w1_hbm,
    w2_hbm,
    sw1_hbm,
    sw2_hbm,
    encoded,
    w1,
    w2,
    sw1,
    sw2,
    outgoing,
    rows_a,
    part_a,
    rs_a,
    ret_a,
    rows_b,
    part_b,
    rs_b,
    ret_b,
    hidden,
    sgather,
    shidden,
    spart,
    sown,
    scross,
    ssum,
    middle,
    sgather_b,
    shidden_b,
    spart_b,
    sown_b,
    scross_b,
    ssum_b,
    middle_b,
    back_a,
    back_b,
    compact,
    spread,
    w_sem,
    local_sem,
    disp_send,
    disp_recv,
    g_send,
    g_recv,
    r_send,
    r_recv,
    ret_send,
    ret_recv,
    sg_send,
    sg_recv,
    sr_send,
    sr_recv,
):
    bf16, f32 = jnp.bfloat16, jnp.float32
    g = lax.axis_index("group")
    w = lax.axis_index("within")
    x, z = lax.rem(w, 2), lax.div(w, 2)
    p = z + x * (7 - 2 * z)

    def device_at(q):
        q = lax.rem(q + 8, 8)
        far = lax.div(q, 4)
        return 2 * q + far * (15 - 4 * q)

    right = (g, device_at(p + 1))
    left = (g, device_at(p - 1))
    yy, core = lax.div(g, 2), lax.rem(g, 2)
    peers = [
        None,
        (2 * yy + 1 - core, w),
        (2 * (1 - yy) + core, w),
        (2 * (1 - yy) + 1 - core, w),
    ]
    barrier = pltpu.get_barrier_semaphore()
    for device in (right, left, peers[1], peers[2], peers[3]):
        pl.semaphore_signal(barrier, inc=1, device_id=device, device_id_type=MESH)

    loads = []
    for i, (src, dst) in enumerate(
        ((w1_hbm, w1), (w2_hbm, w2), (sw1_hbm, sw1), (sw2_hbm, sw2))
    ):
        copy = pltpu.make_async_copy(src, dst, w_sem.at[i])
        copy.start()
        loads.append(copy)

    count = tokens.shape[0]
    cap_a, cap_b = count // 4, count // 8
    late = count // 4
    i0 = lax.broadcasted_iota(jnp.int32, (count, count), 0)
    i1 = lax.broadcasted_iota(jnp.int32, (count, count), 1)
    eye = i0 == i1

    def to_column(row):
        return jnp.sum(jnp.where(eye, row, 0.0), axis=1, keepdims=True)

    def to_row(column):
        return jnp.sum(jnp.where(eye, column, 0.0), axis=0, keepdims=True)

    num_langs = lang_group.shape[1]
    lang = to_column(languages[...].astype(f32))
    lang_ids = lax.broadcasted_iota(jnp.int32, (count, num_langs), 1).astype(f32)
    group_column = jnp.sum(
        jnp.where(lang == lang_ids, lang_group[...].astype(f32), 0.0), axis=1, keepdims=True
    )
    group_row = to_row(group_column)
    same = group_column == group_row
    slot_column = row_sum(same & (i1 < i0))
    slot_row = column_sum(same & (i0 < i1))
    my_y, my_core = yy.astype(f32), core.astype(f32)

    def position(group, slot):
        gy = jnp.where(group >= 2.0, 1.0, 0.0)
        dy, dc = gy - my_y, group - 2.0 * gy - my_core
        r = 2.0 * dy * dy + dc * dc
        return jnp.where(
            slot < cap_a, r * cap_a + slot, count + r * cap_b + slot - cap_a
        )

    place_column = position(group_column, slot_column)
    place_row = position(group_row, slot_row)
    total_slots = 4 * (cap_a + cap_b)
    out_map = (
        lax.broadcasted_iota(jnp.int32, (total_slots, count), 0).astype(f32) == place_row
    )
    normed = layer_norm(
        tokens[...].astype(f32), by_group(group_column, group_gain)
    ).astype(bf16)
    outgoing[...] = jnp.dot(
        jnp.where(out_map, 1.0, 0.0).astype(bf16), normed, preferred_element_type=f32
    ).astype(bf16)
    base = {"a": 0, "b": 4 * cap_a}
    caps = {"a": cap_a, "b": cap_b}
    stage = {"a": 0, "b": 1}
    rows = {"a": rows_a, "b": rows_b}
    part = {"a": part_a, "b": part_b}
    rs = {"a": rs_a, "b": rs_b}
    ret = {"a": ret_a, "b": ret_b}
    own = {}
    for k in "ab":
        own[k] = pltpu.make_async_copy(
            outgoing.at[pl.ds(base[k], caps[k])],
            rows[k].at[pl.ds(0, caps[k])],
            local_sem.at[stage[k]],
        )
        own[k].start()
    pl.semaphore_wait(barrier, 5)

    pending = []

    def send(src, dst, send_sem, recv_sem, device):
        copy = pltpu.make_async_remote_copy(
            src_ref=src,
            dst_ref=dst,
            send_sem=send_sem,
            recv_sem=recv_sem,
            device_id=device,
            device_id_type=MESH,
        )
        copy.start()
        pending.append(copy)
        return copy

    def drain(keep):
        while len(pending) > keep:
            pending.pop(0).wait_send()

    def chunk(k, slot, c):
        return pl.ds((slot * 4 + c) * caps[k], caps[k])

    dispatch = {}
    for k in "ab":
        for r in (2, 3, 1):
            dispatch[k, r] = send(
                outgoing.at[pl.ds(base[k] + r * caps[k], caps[k])],
                rows[k].at[chunk(k, 0, r)],
                disp_send.at[stage[k], r],
                disp_recv.at[stage[k], r],
                peers[r],
            )

    def slot_of(way, s):
        return 7 if s == 4 else (0 if s == 0 else 2 * s - 1 + way)

    arrivals = {}

    def forward(k, way, s, c):
        arrivals[k, way, s + 1, c] = send(
            rows[k].at[chunk(k, slot_of(way, s), c)],
            rows[k].at[chunk(k, slot_of(way, s + 1), c)],
            g_send.at[stage[k], way, s, c],
            g_recv.at[stage[k], way, s + 1, c],
            right if way == 0 else left,
        )

    def first_tiles(k, slot, slots, begin, end):
        size = slots * 4 * caps[k]

        def body(i, carry):
            cols = columns(i, TILE)
            value = jnp.dot(
                rows[k][pl.ds(slot * 4 * caps[k], size), :],
                w1[:, cols],
                preferred_element_type=f32,
            )
            hidden[pl.ds(0, size), cols] = jnp.maximum(value + b1[:, cols], 0.0).astype(bf16)
            return carry

        lax.fori_loop(begin, end, body, 0)

    def second_tiles(k, slot, slots, begin, end):
        size = slots * 4 * caps[k]

        def body(i, carry):
            cols = columns(i, TILE)
            part[k][pl.ds(slot * 4 * caps[k], size), cols] = jnp.dot(
                hidden[pl.ds(0, size), :], w2[:, cols], preferred_element_type=f32
            ).astype(bf16)
            return carry

        lax.fori_loop(begin, end, body, 0)

    n1, n2 = w1.shape[1] // TILE, w2.shape[1] // TILE

    def piece(k, slot, slots, c):
        if c < 2:
            first_tiles(k, slot, slots, c * n1 // 2, (c + 1) * n1 // 2)
        else:
            second_tiles(k, slot, slots, (c - 2) * n2 // 2, (c - 1) * n2 // 2)

    def whole(k, slot, slots):
        first_tiles(k, slot, slots, 0, n1)
        second_tiles(k, slot, slots, 0, n2)

    def gather_start(k):
        own[k].wait()
        for c in range(4):
            if c:
                dispatch[k, c].wait_recv()
            forward(k, 0, 0, c)
            forward(k, 1, 0, c)

    def gather_step(k, s, c):
        for way in (0, 1):
            arrivals[k, way, s, c].wait_recv()
            if s < 3 or c // 2 == way:
                forward(k, way, s, c)

    def rs_slot(way, t):
        return (7, 6 - way, 4 - way, 2 - way)[t]

    def rs_chunk(k, way, t, c):
        at = way * 14 + (c % 2 if t == 0 else 4 * t - 2 + c)
        return pl.ds(at * caps[k], caps[k])

    sums = {}

    def pass_on(k, way, t, c):
        sums[k, way, t, c] = send(
            part[k].at[chunk(k, rs_slot(way, t), c)],
            rs[k].at[rs_chunk(k, way, t, c)],
            r_send.at[stage[k], way, t, c],
            r_recv.at[stage[k], way, t, c],
            right if way == 0 else left,
        )

    def add_in(k, way, t, c):
        sums[k, way, t, c].wait_recv()
        here = chunk(k, rs_slot(way, t + 1), c)
        part[k][here, :] = (
            part[k][here, :].astype(f32) + rs[k][rs_chunk(k, way, t, c), :].astype(f32)
        ).astype(bf16)
        pass_on(k, way, t + 1, c)

    order = (2, 3, 0, 1)

    def reduce_start(k, between):
        for c in (2, 3):
            pass_on(k, 0, 1, c)
            pass_on(k, 1, 1, c - 2)
        between()
        for c in (0, 1):
            arrivals[k, 0, 4, c].wait_recv()
            arrivals[k, 1, 4, c + 2].wait_recv()
        whole(k, 7, 1)
        for c in (0, 1):
            pass_on(k, 0, 0, c)
            pass_on(k, 1, 0, c + 2)
        between()
        for c in (0, 1):
            add_in(k, 0, 0, c)
            add_in(k, 1, 0, c + 2)

    returned = {}

    def reduce_end(k, c):
        sums[k, 0, 3, c].wait_recv()
        sums[k, 1, 3, c].wait_recv()
        here = chunk(k, 0, c)
        total = (
            part[k][here, :].astype(f32)
            + rs[k][rs_chunk(k, 0, 3, c), :].astype(f32)
            + rs[k][rs_chunk(k, 1, 3, c), :].astype(f32)
        ).astype(bf16)
        if c == 0:
            ret[k][pl.ds(0, caps[k]), :] = total
        else:
            part[k][here, :] = total
            returned[k, c] = send(
                part[k].at[here],
                ret[k].at[pl.ds(c * caps[k], caps[k])],
                ret_send.at[stage[k], c],
                ret_recv.at[stage[k], c],
                peers[c],
            )

    m1, m2 = sw1.shape[1] // TILE, sw2.shape[1] // TILE

    def shared_first(source, start, size, target, begin, end):
        def body(i, carry):
            cols = columns(i, TILE)
            value = jnp.dot(
                source[pl.ds(start, size), :], sw1[:, cols], preferred_element_type=f32
            )
            target[:, cols] = jnp.maximum(value + sb1[:, cols], 0.0).astype(bf16)
            return carry

        lax.fori_loop(begin, end, body, 0)

    def shared_second(source, target, start, size, begin, end):
        def body(i, carry):
            cols = columns(i, TILE)
            target[pl.ds(start, size), cols] = jnp.dot(
                source[...], sw2[:, cols], preferred_element_type=f32
            ).astype(bf16)
            return carry

        lax.fori_loop(begin, end, body, 0)

    quarters = 4
    width = sw2.shape[1] // quarters

    def quarter(q):
        return pl.ds(q * width, width)

    def add_crossed(source, cross, target, at, copy, send_sem, recv_sem, q):
        cols = quarter(q)
        copy.wait_recv()
        source[at, cols] = (
            source[at, cols].astype(f32) + cross[:, cols].astype(f32)
        ).astype(bf16)
        return send(source.at[at, cols], target.at[:, cols], send_sem, recv_sem, peers[2])

    def combined(total, own_part, sibling, crossed, cols):
        return (
            total
            + (own_part.astype(f32) + sibling.astype(f32) + crossed.astype(f32))
            + sb2[:, cols]
        )

    half = count // 2

    def block(r, h=None):
        if h is None:
            return pl.ds(r * count, count)
        return pl.ds(r * count + h * half, half)

    def shared_a():
        for c in (1, 2, 3):
            returned["a", c].wait_recv()
        from_sibling, from_y, from_far = [], [], []
        for h in range(2):
            some = pl.ds(h * half, half)
            value = middle[some, :] + jnp.dot(
                back_a[some, :], ret_a[...], preferred_element_type=f32
            )
            middle[some, :] = value
            sgather[some, :] = layer_norm(value, gain2[...]).astype(bf16)
            for r, into in ((2, from_y), (1, from_sibling)):
                into.append(
                    send(
                        sgather.at[some],
                        sgather.at[block(r, h)],
                        sg_send.at[r, h],
                        sg_recv.at[r, h],
                        peers[r],
                    )
                )
        yield
        loads[2].wait()
        loads[3].wait()
        for h in range(2):
            from_sibling[h].wait_recv()
        for q in range(4):
            shared_first(sgather, 0, 2 * count, shidden, q * m1 // 4, (q + 1) * m1 // 4)
            yield
        for q in range(4):
            shared_second(shidden, spart, 0, 2 * count, q * m2 // 4, (q + 1) * m2 // 4)
            yield
        to_own = send(
            spart.at[block(1)], sown, sr_send.at[2, 0], sr_recv.at[2, 0], peers[1]
        )
        yield
        for h in range(2):
            from_y[h].wait_recv()
            from_far.append(
                send(
                    sgather.at[block(2, h)],
                    sgather.at[block(3, h)],
                    sg_send.at[3, h],
                    sg_recv.at[3, h],
                    peers[1],
                )
            )
            yield
        for h in range(2):
            from_far[h].wait_recv()
        for q in range(4):
            shared_first(
                sgather, 2 * count, 2 * count, shidden, q * m1 // 4, (q + 1) * m1 // 4
            )
            yield
        crossed, summed = [], []

        def finish(q):
            summed.append(
                add_crossed(
                    spart, scross, ssum, block(2), crossed[q], sr_send.at[1, q], sr_recv.at[1, q], q
                )
            )

        for q in range(quarters):
            shared_second(
                shidden, spart, 2 * count, 2 * count, q * m2 // 4, (q + 1) * m2 // 4
            )
            crossed.append(
                send(
                    spart.at[block(3), quarter(q)],
                    scross.at[:, quarter(q)],
                    sr_send.at[0, q],
                    sr_recv.at[0, q],
                    peers[1],
                )
            )
            if q:
                finish(q - 1)
            yield
        finish(quarters - 1)
        yield
        to_own.wait_recv()
        for q in range(quarters):
            cols = quarter(q)
            summed[q].wait_recv()
            middle[:, cols] = combined(
                middle[:, cols], spart[block(0), cols], sown[:, cols], ssum[:, cols], cols
            )
            yield

    gather_start("a")
    back_a[...] = jnp.where(
        lax.broadcasted_iota(jnp.int32, (count, 4 * cap_a), 1).astype(f32) == place_column,
        1.0,
        0.0,
    ).astype(bf16)
    middle[...] = tokens[...].astype(f32) + by_group(group_column, group_b2)
    rank_row = column_sum((slot_column >= cap_a) & (i0 < i1))
    rank_row = jnp.where(slot_row >= cap_a, rank_row, -1.0)
    rank_column = row_sum((slot_row >= cap_a) & (i1 < i0))
    rank_column = jnp.where(slot_column >= cap_a, rank_column, -1.0)
    pick = jnp.where(
        lax.broadcasted_iota(jnp.int32, (late, count), 0).astype(f32) == rank_row, 1.0, 0.0
    )
    compact[...] = pick.astype(bf16)
    spread[...] = jnp.where(
        lax.broadcasted_iota(jnp.int32, (count, late), 1).astype(f32) == rank_column, 1.0, 0.0
    ).astype(bf16)
    late_place = jnp.sum(pick * place_row, axis=1, keepdims=True) - 4.0 * cap_a
    late_group = jnp.sum(pick * group_row, axis=1, keepdims=True)
    back_b[...] = jnp.where(
        lax.broadcasted_iota(jnp.int32, (late, 4 * cap_b), 1).astype(f32) == late_place,
        1.0,
        0.0,
    ).astype(bf16)
    middle_b[...] = jnp.dot(
        compact[...], tokens[...], preferred_element_type=f32
    ) + by_group(late_group, group_b2)
    loads[0].wait()
    loads[1].wait()
    for s in (1, 2, 3):
        for c in range(4):
            gather_step("a", s, c)
            if s == 1:
                piece("a", 0, 1, c)
            else:
                piece("a", 2 * s - 3, 2, c)
    gather_start("b")
    whole("a", 5, 2)
    reduce_start("a", lambda: None)
    drain(16)
    for t in (1, 2):
        for c in range(4):
            for way in (0, 1):
                add_in("a", way, t, order[c])
            gather_step("b", t, c)
        if t == 1:
            drain(32)
    for c in range(4):
        reduce_end("a", order[c])
        gather_step("b", 3, c)
        piece("b", 0, 5, c)

    shared = shared_a()

    def go_on():
        next(shared, None)

    go_on()
    whole("b", 5, 2)
    reduce_start("b", go_on)
    for t in (1, 2):
        for c in order:
            for way in (0, 1):
                add_in("b", way, t, c)
            go_on()
    for c in order:
        reduce_end("b", c)
        go_on()
    for _ in range(3):
        go_on()

    for c in (1, 2, 3):
        returned["b", c].wait_recv()

    def block_b(r):
        return pl.ds(r * late, late)

    value = middle_b[...] + jnp.dot(back_b[...], ret_b[...], preferred_element_type=f32)
    middle_b[...] = value
    sgather_b[block_b(0), :] = layer_norm(value, gain2[...]).astype(bf16)
    near = {}
    for r in (2, 1):
        near[r] = send(
            sgather_b.at[block_b(0)],
            sgather_b.at[block_b(r)],
            sg_send.at[r, 2],
            sg_recv.at[r, 2],
            peers[r],
        )
    for _ in shared:
        pass
    drain(16)
    near[2].wait_recv()
    near[3] = send(
        sgather_b.at[block_b(2)],
        sgather_b.at[block_b(3)],
        sg_send.at[3, 2],
        sg_recv.at[3, 2],
        peers[1],
    )
    near[1].wait_recv()
    near[3].wait_recv()
    shared_first(sgather_b, 0, 4 * late, shidden_b, 0, m1)
    crossed, to_own, summed = [], [], []

    def finish_b(q):
        summed.append(
            add_crossed(
                spart_b,
                scross_b,
                ssum_b,
                block_b(2),
                crossed[q],
                sr_send.at[4, q],
                sr_recv.at[4, q],
                q,
            )
        )

    for q in range(quarters):
        cols = quarter(q)
        shared_second(shidden_b, spart_b, 0, 4 * late, q * m2 // 4, (q + 1) * m2 // 4)
        crossed.append(
            send(
                spart_b.at[block_b(3), cols],
                scross_b.at[:, cols],
                sr_send.at[3, q],
                sr_recv.at[3, q],
                peers[1],
            )
        )
        to_own.append(
            send(
                spart_b.at[block_b(1), cols],
                sown_b.at[:, cols],
                sr_send.at[5, q],
                sr_recv.at[5, q],
                peers[1],
            )
        )
        if q:
            finish_b(q - 1)
    finish_b(quarters - 1)
    for q in range(quarters):
        cols = quarter(q)
        to_own[q].wait_recv()
        summed[q].wait_recv()
        late_out = combined(
            middle_b[:, cols], spart_b[block_b(0), cols], sown_b[:, cols], ssum_b[:, cols], cols
        ).astype(bf16)
        placed = jnp.dot(spread[...], late_out, preferred_element_type=f32)
        is_late = jnp.sum(spread[...].astype(f32), axis=1, keepdims=True)
        encoded[:, cols] = jnp.where(is_late > 0.5, placed, middle[:, cols]).astype(bf16)
    drain(0)


def fused_on_device(
    tokens,
    languages,
    lang_group,
    group_gain,
    group_w1,
    group_b1,
    group_w2,
    group_b2,
    shared_gain,
    shared_w1,
    shared_b1,
    shared_w2,
    shared_b2,
):
    count, width = tokens.shape
    unit = group_w1.shape[2]
    shared_unit = shared_w1.shape[1]
    cap_a, cap_b = count // 4, count // 8
    late = count // 4
    bf16, f32 = jnp.bfloat16, jnp.float32
    in_vmem = pl.BlockSpec(memory_space=pltpu.VMEM)
    anywhere = pl.BlockSpec(memory_space=pl.ANY)
    dma = pltpu.SemaphoreType.DMA

    def held(rows, columns=width, dtype=bf16):
        return pltpu.VMEM((rows, columns), dtype)

    return pl.pallas_call(
        fused_kernel,
        out_shape=jax.ShapeDtypeStruct((count, width), bf16),
        in_specs=[in_vmem] * 9 + [anywhere] * 4,
        out_specs=in_vmem,
        scratch_shapes=[
            held(width, unit),
            held(unit),
            held(width, shared_unit),
            held(shared_unit),
            held(4 * (cap_a + cap_b)),
            held(32 * cap_a),
            held(32 * cap_a),
            held(28 * cap_a),
            held(4 * cap_a),
            held(32 * cap_b),
            held(32 * cap_b),
            held(28 * cap_b),
            held(4 * cap_b),
            held(max(8 * cap_a, 20 * cap_b), unit),
            held(4 * count),
            held(2 * count, shared_unit),
            held(4 * count),
            held(count),
            held(count),
            held(count),
            held(count, dtype=f32),
            held(4 * late),
            held(4 * late, shared_unit),
            held(4 * late),
            held(late),
            held(late),
            held(late),
            held(late, dtype=f32),
            held(count, 4 * cap_a),
            held(late, 4 * cap_b),
            held(late, count),
            held(count, late),
            dma((4,)),
            dma((2,)),
            dma((2, 4)),
            dma((2, 4)),
            dma((2, 2, 4, 4)),
            dma((2, 2, 5, 4)),
            dma((2, 2, 4, 4)),
            dma((2, 2, 4, 4)),
            dma((2, 4)),
            dma((2, 4)),
            dma((4, 3)),
            dma((4, 3)),
            dma((6, 4)),
            dma((6, 4)),
        ],
        compiler_params=pltpu.CompilerParams(
            collective_id=0, has_side_effects=True, vmem_limit_bytes=62 * 1024 * 1024
        ),
    )(
        tokens,
        languages[None, :],
        lang_group[None, :],
        group_gain,
        group_b2,
        group_b1,
        shared_gain[None, :],
        shared_b1[None, :],
        shared_b2[None, :],
        group_w1[0],
        group_w2[0],
        shared_w1,
        shared_w2,
    )


def plain_on_device(
    tokens,
    languages,
    lang_group,
    group_gain,
    group_w1,
    group_b1,
    group_w2,
    group_b2,
    shared_gain,
    shared_w1,
    shared_b1,
    shared_w2,
    shared_b2,
):
    tok_dev = tokens.shape[0]
    width_model = tokens.shape[1]
    num_groups = group_gain.shape[0]
    num_langs = lang_group.shape[0]
    capacity = 3 * tok_dev // (2 * lax.axis_size("group"))
    residual_in = tokens.astype(jnp.float32)
    lang_hit = (languages[:, None] == jnp.arange(num_langs, dtype=jnp.int32)[None, :]).astype(
        jnp.int32
    )
    group_of = jnp.sum(lang_hit * lang_group[None, :], axis=1)
    onehot = (group_of[:, None] == jnp.arange(num_groups, dtype=jnp.int32)[None, :]).astype(
        jnp.int32
    )
    earlier = jnp.cumsum(onehot, axis=0) - onehot
    slot_index = jnp.sum(earlier * onehot, axis=1)
    position = group_of * capacity + slot_index
    dispatch_map = (
        position[None, :] == jnp.arange(num_groups * capacity, dtype=jnp.int32)[:, None]
    ).astype(jnp.bfloat16)
    onehot_float = onehot.astype(jnp.float32)
    row_gains = jnp.dot(onehot_float, group_gain, precision=lax.Precision.HIGHEST)
    normed = layer_norm(residual_in, row_gains).astype(jnp.bfloat16)
    outgoing = jnp.dot(dispatch_map, normed, preferred_element_type=jnp.float32).astype(
        jnp.bfloat16
    )
    outgoing = outgoing.reshape(num_groups, capacity, width_model)
    arrived = lax.all_to_all(outgoing, "group", split_axis=0, concat_axis=0, tiled=True)
    group_rows = arrived.reshape(num_groups * capacity, width_model)
    first_proj = group_w1[0]
    first_bias = group_b1[0]
    second_proj = group_w2[0]
    hidden = jax.nn.relu(
        jnp.dot(
            lax.all_gather(group_rows, "within", axis=0, tiled=True),
            first_proj,
            preferred_element_type=jnp.float32,
        )
        + first_bias
    ).astype(jnp.bfloat16)
    selected = hidden
    summed = lax.psum_scatter(
        jnp.dot(selected, second_proj, preferred_element_type=jnp.float32).astype(jnp.bfloat16),
        "within",
        scatter_dimension=0,
        tiled=True,
    )
    returned = lax.all_to_all(
        summed.reshape(num_groups, capacity, width_model),
        "group",
        split_axis=0,
        concat_axis=0,
        tiled=True,
    )
    returned = returned.reshape(num_groups * capacity, width_model)
    group_out = lax.dot_general(
        dispatch_map, returned, (((0,), (0,)), ((), ())), preferred_element_type=jnp.float32
    )
    group_bias = jnp.dot(onehot_float, group_b2, precision=lax.Precision.HIGHEST)
    middle = residual_in + group_out + group_bias
    shared_in = layer_norm(middle, shared_gain).astype(jnp.bfloat16)
    shared_hidden = jax.nn.relu(
        jnp.dot(
            lax.all_gather(shared_in, "group", axis=0, tiled=True),
            shared_w1,
            preferred_element_type=jnp.float32,
        )
        + shared_b1
    ).astype(jnp.bfloat16)
    selected = shared_hidden
    shared_out = lax.psum_scatter(
        jnp.dot(selected, shared_w2, preferred_element_type=jnp.float32).astype(jnp.bfloat16),
        "group",
        scatter_dimension=0,
        tiled=True,
    ).astype(jnp.float32)
    return (middle + shared_out + shared_b2).astype(jnp.bfloat16)


def solution(mesh):
    placed = (
        P(("group", "within"), None),
        P(("group", "within")),
        P(),
        P(),
        P("group", None, "within"),
        P("group", "within"),
        P("group", "within", None),
        P(),
        P(),
        P(None, "group"),
        P("group"),
        P("group", None),
        P(),
    )
    fits = mesh.shape["group"] == 4 and mesh.shape["within"] == 8
    return jax.shard_map(
        fused_on_device if fits else plain_on_device,
        mesh=mesh,
        in_specs=placed,
        out_specs=P(("group", "within"), None),
        check_vma=False,
    )
```

```python
import jax
import jax.numpy as jnp
from jax import lax
from jax.experimental import pallas as pl
from jax.experimental.pallas import tpu as pltpu
from jax.sharding import PartitionSpec as P

MESH = pl.DeviceIdType.MESH
TILE = 512


def layer_norm(values, gains):
    centre = jnp.mean(values, axis=-1, keepdims=True)
    centred = values - centre
    spread = jnp.mean(centred * centred, axis=-1, keepdims=True)
    return centred * lax.rsqrt(spread + 1e-05) * gains


def columns(tile, size):
    return pl.ds(pl.multiple_of(tile * size, size), size)


def row_sum(mask):
    return jnp.sum(jnp.where(mask, 1.0, 0.0), axis=1, keepdims=True)


def column_sum(mask):
    return jnp.sum(jnp.where(mask, 1.0, 0.0), axis=0, keepdims=True)


def by_group(column, table):
    value = jnp.where(column == 0.0, table[0:1, :], 0.0)
    for i in range(1, table.shape[0]):
        value = jnp.where(column == float(i), table[i : i + 1, :], value)
    return value


def fused_kernel(
    tokens,
    languages,
    lang_group,
    group_gain,
    group_b2,
    b1,
    gain2,
    sb1,
    sb2,
    w1_hbm,
    w2_hbm,
    sw1_hbm,
    sw2_hbm,
    encoded,
    w1,
    w2,
    sw1,
    sw2,
    outgoing,
    rows_a,
    part_a,
    rs_a,
    ret_a,
    rows_b,
    part_b,
    rs_b,
    ret_b,
    hidden,
    sgather,
    shidden,
    spart,
    sown,
    scross,
    ssum,
    middle,
    sgather_b,
    shidden_b,
    spart_b,
    sown_b,
    scross_b,
    ssum_b,
    middle_b,
    back_a,
    back_b,
    compact,
    spread,
    w_sem,
    local_sem,
    disp_send,
    disp_recv,
    g_send,
    g_recv,
    r_send,
    r_recv,
    ret_send,
    ret_recv,
    sg_send,
    sg_recv,
    sr_send,
    sr_recv,
):
    bf16, f32 = jnp.bfloat16, jnp.float32
    g = lax.axis_index("group")
    w = lax.axis_index("within")
    x, z = lax.rem(w, 2), lax.div(w, 2)
    p = z + x * (7 - 2 * z)

    def device_at(q):
        q = lax.rem(q + 8, 8)
        far = lax.div(q, 4)
        return 2 * q + far * (15 - 4 * q)

    right = (g, device_at(p + 1))
    left = (g, device_at(p - 1))
    yy, core = lax.div(g, 2), lax.rem(g, 2)
    peers = [
        None,
        (2 * yy + 1 - core, w),
        (2 * (1 - yy) + core, w),
        (2 * (1 - yy) + 1 - core, w),
    ]
    barrier = pltpu.get_barrier_semaphore()
    for device in (right, left, peers[1], peers[2], peers[3]):
        pl.semaphore_signal(barrier, inc=1, device_id=device, device_id_type=MESH)

    loads = []
    for i, (src, dst) in enumerate(
        ((w1_hbm, w1), (w2_hbm, w2), (sw1_hbm, sw1), (sw2_hbm, sw2))
    ):
        copy = pltpu.make_async_copy(src, dst, w_sem.at[i])
        copy.start()
        loads.append(copy)

    count = tokens.shape[0]
    cap_a, cap_b = count // 4, count // 8
    late = count // 4
    i0 = lax.broadcasted_iota(jnp.int32, (count, count), 0)
    i1 = lax.broadcasted_iota(jnp.int32, (count, count), 1)
    eye = i0 == i1

    def to_column(row):
        return jnp.sum(jnp.where(eye, row, 0.0), axis=1, keepdims=True)

    def to_row(column):
        return jnp.sum(jnp.where(eye, column, 0.0), axis=0, keepdims=True)

    num_langs = lang_group.shape[1]
    lang = to_column(languages[...].astype(f32))
    lang_ids = lax.broadcasted_iota(jnp.int32, (count, num_langs), 1).astype(f32)
    group_column = jnp.sum(
        jnp.where(lang == lang_ids, lang_group[...].astype(f32), 0.0), axis=1, keepdims=True
    )
    group_row = to_row(group_column)
    same = group_column == group_row
    slot_column = row_sum(same & (i1 < i0))
    slot_row = column_sum(same & (i0 < i1))
    my_y, my_core = yy.astype(f32), core.astype(f32)

    def position(group, slot):
        gy = jnp.where(group >= 2.0, 1.0, 0.0)
        dy, dc = gy - my_y, group - 2.0 * gy - my_core
        r = 2.0 * dy * dy + dc * dc
        return jnp.where(
            slot < cap_a, r * cap_a + slot, count + r * cap_b + slot - cap_a
        )

    place_column = position(group_column, slot_column)
    place_row = position(group_row, slot_row)
    total_slots = 4 * (cap_a + cap_b)
    out_map = (
        lax.broadcasted_iota(jnp.int32, (total_slots, count), 0).astype(f32) == place_row
    )
    normed = layer_norm(
        tokens[...].astype(f32), by_group(group_column, group_gain)
    ).astype(bf16)
    outgoing[...] = jnp.dot(
        jnp.where(out_map, 1.0, 0.0).astype(bf16), normed, preferred_element_type=f32
    ).astype(bf16)
    base = {"a": 0, "b": 4 * cap_a}
    caps = {"a": cap_a, "b": cap_b}
    stage = {"a": 0, "b": 1}
    rows = {"a": rows_a, "b": rows_b}
    part = {"a": part_a, "b": part_b}
    rs = {"a": rs_a, "b": rs_b}
    ret = {"a": ret_a, "b": ret_b}
    own = {}
    for k in "ab":
        own[k] = pltpu.make_async_copy(
            outgoing.at[pl.ds(base[k], caps[k])],
            rows[k].at[pl.ds(0, caps[k])],
            local_sem.at[stage[k]],
        )
        own[k].start()
    pl.semaphore_wait(barrier, 5)

    pending = []

    def send(src, dst, send_sem, recv_sem, device):
        copy = pltpu.make_async_remote_copy(
            src_ref=src,
            dst_ref=dst,
            send_sem=send_sem,
            recv_sem=recv_sem,
            device_id=device,
            device_id_type=MESH,
        )
        copy.start()
        pending.append(copy)
        return copy

    def drain(keep):
        while len(pending) > keep:
            pending.pop(0).wait_send()

    def chunk(k, slot, c):
        return pl.ds((slot * 4 + c) * caps[k], caps[k])

    dispatch = {}
    for k in "ab":
        for r in (2, 3, 1):
            dispatch[k, r] = send(
                outgoing.at[pl.ds(base[k] + r * caps[k], caps[k])],
                rows[k].at[chunk(k, 0, r)],
                disp_send.at[stage[k], r],
                disp_recv.at[stage[k], r],
                peers[r],
            )

    def slot_of(way, s):
        return 7 if s == 4 else (0 if s == 0 else 2 * s - 1 + way)

    arrivals = {}

    def forward(k, way, s, c):
        arrivals[k, way, s + 1, c] = send(
            rows[k].at[chunk(k, slot_of(way, s), c)],
            rows[k].at[chunk(k, slot_of(way, s + 1), c)],
            g_send.at[stage[k], way, s, c],
            g_recv.at[stage[k], way, s + 1, c],
            right if way == 0 else left,
        )

    def first_tiles(k, slot, slots, begin, end):
        size = slots * 4 * caps[k]

        def body(i, carry):
            cols = columns(i, TILE)
            value = jnp.dot(
                rows[k][pl.ds(slot * 4 * caps[k], size), :],
                w1[:, cols],
                preferred_element_type=f32,
            )
            hidden[pl.ds(0, size), cols] = jnp.maximum(value + b1[:, cols], 0.0).astype(bf16)
            return carry

        lax.fori_loop(begin, end, body, 0)

    def second_tiles(k, slot, slots, begin, end):
        size = slots * 4 * caps[k]

        def body(i, carry):
            cols = columns(i, TILE)
            part[k][pl.ds(slot * 4 * caps[k], size), cols] = jnp.dot(
                hidden[pl.ds(0, size), :], w2[:, cols], preferred_element_type=f32
            ).astype(bf16)
            return carry

        lax.fori_loop(begin, end, body, 0)

    n1, n2 = w1.shape[1] // TILE, w2.shape[1] // TILE

    def piece(k, slot, slots, c):
        if c < 2:
            first_tiles(k, slot, slots, c * n1 // 2, (c + 1) * n1 // 2)
        else:
            second_tiles(k, slot, slots, (c - 2) * n2 // 2, (c - 1) * n2 // 2)

    def whole(k, slot, slots):
        first_tiles(k, slot, slots, 0, n1)
        second_tiles(k, slot, slots, 0, n2)

    def gather_start(k):
        own[k].wait()
        for c in range(4):
            if c:
                dispatch[k, c].wait_recv()
            forward(k, 0, 0, c)
            forward(k, 1, 0, c)

    def gather_step(k, s, c):
        for way in (0, 1):
            arrivals[k, way, s, c].wait_recv()
            if s < 3 or c // 2 == way:
                forward(k, way, s, c)

    def rs_slot(way, t):
        return (7, 6 - way, 4 - way, 2 - way)[t]

    def rs_chunk(k, way, t, c):
        at = way * 14 + (c % 2 if t == 0 else 4 * t - 2 + c)
        return pl.ds(at * caps[k], caps[k])

    sums = {}

    def pass_on(k, way, t, c):
        sums[k, way, t, c] = send(
            part[k].at[chunk(k, rs_slot(way, t), c)],
            rs[k].at[rs_chunk(k, way, t, c)],
            r_send.at[stage[k], way, t, c],
            r_recv.at[stage[k], way, t, c],
            right if way == 0 else left,
        )

    def add_in(k, way, t, c):
        sums[k, way, t, c].wait_recv()
        here = chunk(k, rs_slot(way, t + 1), c)
        part[k][here, :] = (
            part[k][here, :].astype(f32) + rs[k][rs_chunk(k, way, t, c), :].astype(f32)
        ).astype(bf16)
        pass_on(k, way, t + 1, c)

    order = (2, 3, 0, 1)

    def reduce_start(k, between):
        for c in (2, 3):
            pass_on(k, 0, 1, c)
            pass_on(k, 1, 1, c - 2)
        between()
        for c in (0, 1):
            arrivals[k, 0, 4, c].wait_recv()
            arrivals[k, 1, 4, c + 2].wait_recv()
        whole(k, 7, 1)
        for c in (0, 1):
            pass_on(k, 0, 0, c)
            pass_on(k, 1, 0, c + 2)
        between()
        for c in (0, 1):
            add_in(k, 0, 0, c)
            add_in(k, 1, 0, c + 2)

    returned = {}

    def reduce_end(k, c):
        sums[k, 0, 3, c].wait_recv()
        sums[k, 1, 3, c].wait_recv()
        here = chunk(k, 0, c)
        total = (
            part[k][here, :].astype(f32)
            + rs[k][rs_chunk(k, 0, 3, c), :].astype(f32)
            + rs[k][rs_chunk(k, 1, 3, c), :].astype(f32)
        ).astype(bf16)
        if c == 0:
            ret[k][pl.ds(0, caps[k]), :] = total
        else:
            part[k][here, :] = total
            returned[k, c] = send(
                part[k].at[here],
                ret[k].at[pl.ds(c * caps[k], caps[k])],
                ret_send.at[stage[k], c],
                ret_recv.at[stage[k], c],
                peers[c],
            )

    m1, m2 = sw1.shape[1] // TILE, sw2.shape[1] // TILE

    def shared_first(source, start, size, target, begin, end):
        def body(i, carry):
            cols = columns(i, TILE)
            value = jnp.dot(
                source[pl.ds(start, size), :], sw1[:, cols], preferred_element_type=f32
            )
            target[:, cols] = jnp.maximum(value + sb1[:, cols], 0.0).astype(bf16)
            return carry

        lax.fori_loop(begin, end, body, 0)

    def shared_second(source, target, start, size, begin, end):
        def body(i, carry):
            cols = columns(i, TILE)
            target[pl.ds(start, size), cols] = jnp.dot(
                source[...], sw2[:, cols], preferred_element_type=f32
            ).astype(bf16)
            return carry

        lax.fori_loop(begin, end, body, 0)

    quarters = 4
    width = sw2.shape[1] // quarters

    def quarter(q):
        return pl.ds(q * width, width)

    def add_crossed(source, cross, target, at, copy, send_sem, recv_sem, q):
        cols = quarter(q)
        copy.wait_recv()
        source[at, cols] = (
            source[at, cols].astype(f32) + cross[:, cols].astype(f32)
        ).astype(bf16)
        return send(source.at[at, cols], target.at[:, cols], send_sem, recv_sem, peers[2])

    def combined(total, own_part, sibling, crossed, cols):
        return (
            total
            + (own_part.astype(f32) + sibling.astype(f32) + crossed.astype(f32))
            + sb2[:, cols]
        )

    half = count // 2

    def block(r, h=None):
        if h is None:
            return pl.ds(r * count, count)
        return pl.ds(r * count + h * half, half)

    def shared_a():
        for c in (1, 2, 3):
            returned["a", c].wait_recv()
        from_sibling, from_y, from_far = [], [], []
        for h in range(2):
            some = pl.ds(h * half, half)
            value = middle[some, :] + jnp.dot(
                back_a[some, :], ret_a[...], preferred_element_type=f32
            )
            middle[some, :] = value
            sgather[some, :] = layer_norm(value, gain2[...]).astype(bf16)
            for r, into in ((2, from_y), (1, from_sibling)):
                into.append(
                    send(
                        sgather.at[some],
                        sgather.at[block(r, h)],
                        sg_send.at[r, h],
                        sg_recv.at[r, h],
                        peers[r],
                    )
                )
        yield
        loads[2].wait()
        loads[3].wait()
        for h in range(2):
            from_sibling[h].wait_recv()
        for q in range(4):
            shared_first(sgather, 0, 2 * count, shidden, q * m1 // 4, (q + 1) * m1 // 4)
            yield
        for q in range(4):
            shared_second(shidden, spart, 0, 2 * count, q * m2 // 4, (q + 1) * m2 // 4)
            yield
        to_own = send(
            spart.at[block(1)], sown, sr_send.at[2, 0], sr_recv.at[2, 0], peers[1]
        )
        yield
        for h in range(2):
            from_y[h].wait_recv()
            from_far.append(
                send(
                    sgather.at[block(2, h)],
                    sgather.at[block(3, h)],
                    sg_send.at[3, h],
                    sg_recv.at[3, h],
                    peers[1],
                )
            )
            yield
        for h in range(2):
            from_far[h].wait_recv()
        for q in range(4):
            shared_first(
                sgather, 2 * count, 2 * count, shidden, q * m1 // 4, (q + 1) * m1 // 4
            )
            yield
        crossed, summed = [], []

        def finish(q):
            summed.append(
                add_crossed(
                    spart, scross, ssum, block(2), crossed[q], sr_send.at[1, q], sr_recv.at[1, q], q
                )
            )

        for q in range(quarters):
            shared_second(
                shidden, spart, 2 * count, 2 * count, q * m2 // 4, (q + 1) * m2 // 4
            )
            crossed.append(
                send(
                    spart.at[block(3), quarter(q)],
                    scross.at[:, quarter(q)],
                    sr_send.at[0, q],
                    sr_recv.at[0, q],
                    peers[1],
                )
            )
            if q:
                finish(q - 1)
            yield
        finish(quarters - 1)
        yield
        to_own.wait_recv()
        for q in range(quarters):
            cols = quarter(q)
            summed[q].wait_recv()
            middle[:, cols] = combined(
                middle[:, cols], spart[block(0), cols], sown[:, cols], ssum[:, cols], cols
            )
            yield

    gather_start("a")
    back_a[...] = jnp.where(
        lax.broadcasted_iota(jnp.int32, (count, 4 * cap_a), 1).astype(f32) == place_column,
        1.0,
        0.0,
    ).astype(bf16)
    middle[...] = tokens[...].astype(f32) + by_group(group_column, group_b2)
    rank_row = column_sum((slot_column >= cap_a) & (i0 < i1))
    rank_row = jnp.where(slot_row >= cap_a, rank_row, -1.0)
    rank_column = row_sum((slot_row >= cap_a) & (i1 < i0))
    rank_column = jnp.where(slot_column >= cap_a, rank_column, -1.0)
    pick = jnp.where(
        lax.broadcasted_iota(jnp.int32, (late, count), 0).astype(f32) == rank_row, 1.0, 0.0
    )
    compact[...] = pick.astype(bf16)
    spread[...] = jnp.where(
        lax.broadcasted_iota(jnp.int32, (count, late), 1).astype(f32) == rank_column, 1.0, 0.0
    ).astype(bf16)
    late_place = jnp.sum(pick * place_row, axis=1, keepdims=True) - 4.0 * cap_a
    late_group = jnp.sum(pick * group_row, axis=1, keepdims=True)
    back_b[...] = jnp.where(
        lax.broadcasted_iota(jnp.int32, (late, 4 * cap_b), 1).astype(f32) == late_place,
        1.0,
        0.0,
    ).astype(bf16)
    middle_b[...] = jnp.dot(
        compact[...], tokens[...], preferred_element_type=f32
    ) + by_group(late_group, group_b2)
    loads[0].wait()
    loads[1].wait()
    for s in (1, 2, 3):
        for c in range(4):
            gather_step("a", s, c)
            if s == 1:
                piece("a", 0, 1, c)
            else:
                piece("a", 2 * s - 3, 2, c)
    gather_start("b")
    whole("a", 5, 2)
    reduce_start("a", lambda: None)
    drain(16)
    for t in (1, 2):
        for c in range(4):
            for way in (0, 1):
                add_in("a", way, t, order[c])
            if t == 2:
                gather_step("b", 1, c)
        if t == 1:
            drain(32)
    for c in order:
        reduce_end("a", c)

    shared = shared_a()

    def go_on():
        next(shared, None)

    for s in (2, 3):
        for c in range(4):
            gather_step("b", s, c)
            go_on()
            if s == 3:
                piece("b", 0, 5, c)
    whole("b", 5, 2)
    reduce_start("b", go_on)
    for t in (1, 2):
        for c in order:
            for way in (0, 1):
                add_in("b", way, t, c)
            go_on()
    for c in order:
        reduce_end("b", c)
        go_on()
    for _ in range(3):
        go_on()

    for c in (1, 2, 3):
        returned["b", c].wait_recv()

    def block_b(r):
        return pl.ds(r * late, late)

    value = middle_b[...] + jnp.dot(back_b[...], ret_b[...], preferred_element_type=f32)
    middle_b[...] = value
    sgather_b[block_b(0), :] = layer_norm(value, gain2[...]).astype(bf16)
    near = {}
    for r in (2, 1):
        near[r] = send(
            sgather_b.at[block_b(0)],
            sgather_b.at[block_b(r)],
            sg_send.at[r, 2],
            sg_recv.at[r, 2],
            peers[r],
        )
    for _ in shared:
        pass
    drain(16)
    near[2].wait_recv()
    near[3] = send(
        sgather_b.at[block_b(2)],
        sgather_b.at[block_b(3)],
        sg_send.at[3, 2],
        sg_recv.at[3, 2],
        peers[1],
    )
    near[1].wait_recv()
    near[3].wait_recv()
    shared_first(sgather_b, 0, 4 * late, shidden_b, 0, m1)
    crossed, to_own, summed = [], [], []

    def finish_b(q):
        summed.append(
            add_crossed(
                spart_b,
                scross_b,
                ssum_b,
                block_b(2),
                crossed[q],
                sr_send.at[4, q],
                sr_recv.at[4, q],
                q,
            )
        )

    for q in range(quarters):
        cols = quarter(q)
        shared_second(shidden_b, spart_b, 0, 4 * late, q * m2 // 4, (q + 1) * m2 // 4)
        crossed.append(
            send(
                spart_b.at[block_b(3), cols],
                scross_b.at[:, cols],
                sr_send.at[3, q],
                sr_recv.at[3, q],
                peers[1],
            )
        )
        to_own.append(
            send(
                spart_b.at[block_b(1), cols],
                sown_b.at[:, cols],
                sr_send.at[5, q],
                sr_recv.at[5, q],
                peers[1],
            )
        )
        if q:
            finish_b(q - 1)
    finish_b(quarters - 1)
    for q in range(quarters):
        cols = quarter(q)
        to_own[q].wait_recv()
        summed[q].wait_recv()
        late_out = combined(
            middle_b[:, cols], spart_b[block_b(0), cols], sown_b[:, cols], ssum_b[:, cols], cols
        ).astype(bf16)
        placed = jnp.dot(spread[...], late_out, preferred_element_type=f32)
        is_late = jnp.sum(spread[...].astype(f32), axis=1, keepdims=True)
        encoded[:, cols] = jnp.where(is_late > 0.5, placed, middle[:, cols]).astype(bf16)
    drain(0)


def fused_on_device(
    tokens,
    languages,
    lang_group,
    group_gain,
    group_w1,
    group_b1,
    group_w2,
    group_b2,
    shared_gain,
    shared_w1,
    shared_b1,
    shared_w2,
    shared_b2,
):
    count, width = tokens.shape
    unit = group_w1.shape[2]
    shared_unit = shared_w1.shape[1]
    cap_a, cap_b = count // 4, count // 8
    late = count // 4
    bf16, f32 = jnp.bfloat16, jnp.float32
    in_vmem = pl.BlockSpec(memory_space=pltpu.VMEM)
    anywhere = pl.BlockSpec(memory_space=pl.ANY)
    dma = pltpu.SemaphoreType.DMA

    def held(rows, columns=width, dtype=bf16):
        return pltpu.VMEM((rows, columns), dtype)

    return pl.pallas_call(
        fused_kernel,
        out_shape=jax.ShapeDtypeStruct((count, width), bf16),
        in_specs=[in_vmem] * 9 + [anywhere] * 4,
        out_specs=in_vmem,
        scratch_shapes=[
            held(width, unit),
            held(unit),
            held(width, shared_unit),
            held(shared_unit),
            held(4 * (cap_a + cap_b)),
            held(32 * cap_a),
            held(32 * cap_a),
            held(28 * cap_a),
            held(4 * cap_a),
            held(32 * cap_b),
            held(32 * cap_b),
            held(28 * cap_b),
            held(4 * cap_b),
            held(max(8 * cap_a, 20 * cap_b), unit),
            held(4 * count),
            held(2 * count, shared_unit),
            held(4 * count),
            held(count),
            held(count),
            held(count),
            held(count, dtype=f32),
            held(4 * late),
            held(4 * late, shared_unit),
            held(4 * late),
            held(late),
            held(late),
            held(late),
            held(late, dtype=f32),
            held(count, 4 * cap_a),
            held(late, 4 * cap_b),
            held(late, count),
            held(count, late),
            dma((4,)),
            dma((2,)),
            dma((2, 4)),
            dma((2, 4)),
            dma((2, 2, 4, 4)),
            dma((2, 2, 5, 4)),
            dma((2, 2, 4, 4)),
            dma((2, 2, 4, 4)),
            dma((2, 4)),
            dma((2, 4)),
            dma((4, 3)),
            dma((4, 3)),
            dma((6, 4)),
            dma((6, 4)),
        ],
        compiler_params=pltpu.CompilerParams(
            collective_id=0, has_side_effects=True, vmem_limit_bytes=62 * 1024 * 1024
        ),
    )(
        tokens,
        languages[None, :],
        lang_group[None, :],
        group_gain,
        group_b2,
        group_b1,
        shared_gain[None, :],
        shared_b1[None, :],
        shared_b2[None, :],
        group_w1[0],
        group_w2[0],
        shared_w1,
        shared_w2,
    )


def plain_on_device(
    tokens,
    languages,
    lang_group,
    group_gain,
    group_w1,
    group_b1,
    group_w2,
    group_b2,
    shared_gain,
    shared_w1,
    shared_b1,
    shared_w2,
    shared_b2,
):
    tok_dev = tokens.shape[0]
    width_model = tokens.shape[1]
    num_groups = group_gain.shape[0]
    num_langs = lang_group.shape[0]
    capacity = 3 * tok_dev // (2 * lax.axis_size("group"))
    residual_in = tokens.astype(jnp.float32)
    lang_hit = (languages[:, None] == jnp.arange(num_langs, dtype=jnp.int32)[None, :]).astype(
        jnp.int32
    )
    group_of = jnp.sum(lang_hit * lang_group[None, :], axis=1)
    onehot = (group_of[:, None] == jnp.arange(num_groups, dtype=jnp.int32)[None, :]).astype(
        jnp.int32
    )
    earlier = jnp.cumsum(onehot, axis=0) - onehot
    slot_index = jnp.sum(earlier * onehot, axis=1)
    position = group_of * capacity + slot_index
    dispatch_map = (
        position[None, :] == jnp.arange(num_groups * capacity, dtype=jnp.int32)[:, None]
    ).astype(jnp.bfloat16)
    onehot_float = onehot.astype(jnp.float32)
    row_gains = jnp.dot(onehot_float, group_gain, precision=lax.Precision.HIGHEST)
    normed = layer_norm(residual_in, row_gains).astype(jnp.bfloat16)
    outgoing = jnp.dot(dispatch_map, normed, preferred_element_type=jnp.float32).astype(
        jnp.bfloat16
    )
    outgoing = outgoing.reshape(num_groups, capacity, width_model)
    arrived = lax.all_to_all(outgoing, "group", split_axis=0, concat_axis=0, tiled=True)
    group_rows = arrived.reshape(num_groups * capacity, width_model)
    first_proj = group_w1[0]
    first_bias = group_b1[0]
    second_proj = group_w2[0]
    hidden = jax.nn.relu(
        jnp.dot(
            lax.all_gather(group_rows, "within", axis=0, tiled=True),
            first_proj,
            preferred_element_type=jnp.float32,
        )
        + first_bias
    ).astype(jnp.bfloat16)
    selected = hidden
    summed = lax.psum_scatter(
        jnp.dot(selected, second_proj, preferred_element_type=jnp.float32).astype(jnp.bfloat16),
        "within",
        scatter_dimension=0,
        tiled=True,
    )
    returned = lax.all_to_all(
        summed.reshape(num_groups, capacity, width_model),
        "group",
        split_axis=0,
        concat_axis=0,
        tiled=True,
    )
    returned = returned.reshape(num_groups * capacity, width_model)
    group_out = lax.dot_general(
        dispatch_map, returned, (((0,), (0,)), ((), ())), preferred_element_type=jnp.float32
    )
    group_bias = jnp.dot(onehot_float, group_b2, precision=lax.Precision.HIGHEST)
    middle = residual_in + group_out + group_bias
    shared_in = layer_norm(middle, shared_gain).astype(jnp.bfloat16)
    shared_hidden = jax.nn.relu(
        jnp.dot(
            lax.all_gather(shared_in, "group", axis=0, tiled=True),
            shared_w1,
            preferred_element_type=jnp.float32,
        )
        + shared_b1
    ).astype(jnp.bfloat16)
    selected = shared_hidden
    shared_out = lax.psum_scatter(
        jnp.dot(selected, shared_w2, preferred_element_type=jnp.float32).astype(jnp.bfloat16),
        "group",
        scatter_dimension=0,
        tiled=True,
    ).astype(jnp.float32)
    return (middle + shared_out + shared_b2).astype(jnp.bfloat16)


def solution(mesh):
    placed = (
        P(("group", "within"), None),
        P(("group", "within")),
        P(),
        P(),
        P("group", None, "within"),
        P("group", "within"),
        P("group", "within", None),
        P(),
        P(),
        P(None, "group"),
        P("group"),
        P("group", None),
        P(),
    )
    fits = mesh.shape["group"] == 4 and mesh.shape["within"] == 8
    return jax.shard_map(
        fused_on_device if fits else plain_on_device,
        mesh=mesh,
        in_specs=placed,
        out_specs=P(("group", "within"), None),
        check_vma=False,
    )
```

```python
import jax
import jax.numpy as jnp
from jax import lax
from jax.experimental import pallas as pl
from jax.experimental.pallas import tpu as pltpu
from jax.sharding import PartitionSpec as P

MESH = pl.DeviceIdType.MESH
TILE = 512


def layer_norm(values, gains):
    centre = jnp.mean(values, axis=-1, keepdims=True)
    centred = values - centre
    spread = jnp.mean(centred * centred, axis=-1, keepdims=True)
    return centred * lax.rsqrt(spread + 1e-05) * gains


def columns(tile, size):
    return pl.ds(pl.multiple_of(tile * size, size), size)


def row_sum(mask):
    return jnp.sum(jnp.where(mask, 1.0, 0.0), axis=1, keepdims=True)


def column_sum(mask):
    return jnp.sum(jnp.where(mask, 1.0, 0.0), axis=0, keepdims=True)


def by_group(column, table):
    value = jnp.where(column == 0.0, table[0:1, :], 0.0)
    for i in range(1, table.shape[0]):
        value = jnp.where(column == float(i), table[i : i + 1, :], value)
    return value


def fused_kernel(
    tokens,
    languages,
    lang_group,
    group_gain,
    group_b2,
    b1,
    gain2,
    sb1,
    sb2,
    w1_hbm,
    w2_hbm,
    sw1_hbm,
    sw2_hbm,
    encoded,
    w1,
    w2,
    sw1,
    sw2,
    outgoing,
    rows_a,
    part_a,
    rs_a,
    ret_a,
    rows_b,
    part_b,
    rs_b,
    ret_b,
    hidden,
    sgather,
    shidden,
    spart,
    sown,
    scross,
    ssum,
    middle,
    sgather_b,
    shidden_b,
    spart_b,
    sown_b,
    scross_b,
    ssum_b,
    middle_b,
    back_a,
    back_b,
    compact,
    spread,
    w_sem,
    local_sem,
    disp_send,
    disp_recv,
    g_send,
    g_recv,
    r_send,
    r_recv,
    ret_send,
    ret_recv,
    sg_send,
    sg_recv,
    sr_send,
    sr_recv,
):
    bf16, f32 = jnp.bfloat16, jnp.float32
    g = lax.axis_index("group")
    w = lax.axis_index("within")
    x, z = lax.rem(w, 2), lax.div(w, 2)
    p = z + x * (7 - 2 * z)

    def device_at(q):
        q = lax.rem(q + 8, 8)
        far = lax.div(q, 4)
        return 2 * q + far * (15 - 4 * q)

    right = (g, device_at(p + 1))
    left = (g, device_at(p - 1))
    yy, core = lax.div(g, 2), lax.rem(g, 2)
    peers = [
        None,
        (2 * yy + 1 - core, w),
        (2 * (1 - yy) + core, w),
        (2 * (1 - yy) + 1 - core, w),
    ]
    barrier = pltpu.get_barrier_semaphore()
    for device in (right, left, peers[1], peers[2], peers[3]):
        pl.semaphore_signal(barrier, inc=1, device_id=device, device_id_type=MESH)

    loads = []
    for i, (src, dst) in enumerate(
        ((w1_hbm, w1), (w2_hbm, w2), (sw1_hbm, sw1), (sw2_hbm, sw2))
    ):
        copy = pltpu.make_async_copy(src, dst, w_sem.at[i])
        copy.start()
        loads.append(copy)

    count = tokens.shape[0]
    cap_a, cap_b = count // 4, count // 8
    late = count // 4
    i0 = lax.broadcasted_iota(jnp.int32, (count, count), 0)
    i1 = lax.broadcasted_iota(jnp.int32, (count, count), 1)
    eye = i0 == i1

    def to_column(row):
        return jnp.sum(jnp.where(eye, row, 0.0), axis=1, keepdims=True)

    def to_row(column):
        return jnp.sum(jnp.where(eye, column, 0.0), axis=0, keepdims=True)

    num_langs = lang_group.shape[1]
    lang = to_column(languages[...].astype(f32))
    lang_ids = lax.broadcasted_iota(jnp.int32, (count, num_langs), 1).astype(f32)
    group_column = jnp.sum(
        jnp.where(lang == lang_ids, lang_group[...].astype(f32), 0.0), axis=1, keepdims=True
    )
    group_row = to_row(group_column)
    same = group_column == group_row
    slot_column = row_sum(same & (i1 < i0))
    slot_row = column_sum(same & (i0 < i1))
    my_y, my_core = yy.astype(f32), core.astype(f32)

    def position(group, slot):
        gy = jnp.where(group >= 2.0, 1.0, 0.0)
        dy, dc = gy - my_y, group - 2.0 * gy - my_core
        r = 2.0 * dy * dy + dc * dc
        return jnp.where(
            slot < cap_a, r * cap_a + slot, count + r * cap_b + slot - cap_a
        )

    place_column = position(group_column, slot_column)
    place_row = position(group_row, slot_row)
    total_slots = 4 * (cap_a + cap_b)
    out_map = (
        lax.broadcasted_iota(jnp.int32, (total_slots, count), 0).astype(f32) == place_row
    )
    normed = layer_norm(
        tokens[...].astype(f32), by_group(group_column, group_gain)
    ).astype(bf16)
    outgoing[...] = jnp.dot(
        jnp.where(out_map, 1.0, 0.0).astype(bf16), normed, preferred_element_type=f32
    ).astype(bf16)
    base = {"a": 0, "b": 4 * cap_a}
    caps = {"a": cap_a, "b": cap_b}
    stage = {"a": 0, "b": 1}
    rows = {"a": rows_a, "b": rows_b}
    part = {"a": part_a, "b": part_b}
    rs = {"a": rs_a, "b": rs_b}
    ret = {"a": ret_a, "b": ret_b}
    own = {}
    for k in "ab":
        own[k] = pltpu.make_async_copy(
            outgoing.at[pl.ds(base[k], caps[k])],
            rows[k].at[pl.ds(0, caps[k])],
            local_sem.at[stage[k]],
        )
        own[k].start()
    pl.semaphore_wait(barrier, 5)

    pending = []

    def send(src, dst, send_sem, recv_sem, device):
        copy = pltpu.make_async_remote_copy(
            src_ref=src,
            dst_ref=dst,
            send_sem=send_sem,
            recv_sem=recv_sem,
            device_id=device,
            device_id_type=MESH,
        )
        copy.start()
        pending.append(copy)
        return copy

    def drain(keep):
        while len(pending) > keep:
            pending.pop(0).wait_send()

    def chunk(k, slot, c):
        return pl.ds((slot * 4 + 2 * c) * caps[k], 2 * caps[k])

    dispatch = {}
    for k in "ab":
        for r in (2, 3, 1):
            dispatch[k, r] = send(
                outgoing.at[pl.ds(base[k] + r * caps[k], caps[k])],
                rows[k].at[pl.ds(r * caps[k], caps[k])],
                disp_send.at[stage[k], r],
                disp_recv.at[stage[k], r],
                peers[r],
            )

    def slot_of(way, s):
        return 7 if s == 4 else (0 if s == 0 else 2 * s - 1 + way)

    arrivals = {}

    def forward(k, way, s, c):
        arrivals[k, way, s + 1, c] = send(
            rows[k].at[chunk(k, slot_of(way, s), c)],
            rows[k].at[chunk(k, slot_of(way, s + 1), c)],
            g_send.at[stage[k], way, s, c],
            g_recv.at[stage[k], way, s + 1, c],
            right if way == 0 else left,
        )

    def first_tiles(k, slot, slots, begin, end):
        size = slots * 4 * caps[k]

        def body(i, carry):
            cols = columns(i, TILE)
            value = jnp.dot(
                rows[k][pl.ds(slot * 4 * caps[k], size), :],
                w1[:, cols],
                preferred_element_type=f32,
            )
            hidden[pl.ds(0, size), cols] = jnp.maximum(value + b1[:, cols], 0.0).astype(bf16)
            return carry

        lax.fori_loop(begin, end, body, 0)

    def second_tiles(k, slot, slots, begin, end):
        size = slots * 4 * caps[k]

        def body(i, carry):
            cols = columns(i, TILE)
            part[k][pl.ds(slot * 4 * caps[k], size), cols] = jnp.dot(
                hidden[pl.ds(0, size), :], w2[:, cols], preferred_element_type=f32
            ).astype(bf16)
            return carry

        lax.fori_loop(begin, end, body, 0)

    n1, n2 = w1.shape[1] // TILE, w2.shape[1] // TILE

    def piece(k, slot, slots, c):
        if c < 2:
            first_tiles(k, slot, slots, c * n1 // 2, (c + 1) * n1 // 2)
        else:
            second_tiles(k, slot, slots, (c - 2) * n2 // 2, (c - 1) * n2 // 2)

    def whole(k, slot, slots):
        first_tiles(k, slot, slots, 0, n1)
        second_tiles(k, slot, slots, 0, n2)

    def gather_start(k):
        own[k].wait()
        for c in range(2):
            for r in (2 * c, 2 * c + 1):
                if r:
                    dispatch[k, r].wait_recv()
            forward(k, 0, 0, c)
            forward(k, 1, 0, c)

    def gather_step(k, s, c):
        for way in (0, 1):
            arrivals[k, way, s, c].wait_recv()
            if s < 3 or c == way:
                forward(k, way, s, c)

    def rs_slot(way, t):
        return (7, 6 - way, 4 - way, 2 - way)[t]

    def rs_chunk(k, way, t, c):
        at = way * 14 + (0 if t == 0 else 4 * t - 2 + 2 * c)
        return pl.ds(at * caps[k], 2 * caps[k])

    sums = {}

    def pass_on(k, way, t, c):
        sums[k, way, t, c] = send(
            part[k].at[chunk(k, rs_slot(way, t), c)],
            rs[k].at[rs_chunk(k, way, t, c)],
            r_send.at[stage[k], way, t, c],
            r_recv.at[stage[k], way, t, c],
            right if way == 0 else left,
        )

    def add_in(k, way, t, c):
        sums[k, way, t, c].wait_recv()
        here = chunk(k, rs_slot(way, t + 1), c)
        part[k][here, :] = (
            part[k][here, :].astype(f32) + rs[k][rs_chunk(k, way, t, c), :].astype(f32)
        ).astype(bf16)
        pass_on(k, way, t + 1, c)

    order = (1, 0)

    def reduce_start(k, between):
        pass_on(k, 0, 1, 1)
        pass_on(k, 1, 1, 0)
        between()
        arrivals[k, 0, 4, 0].wait_recv()
        arrivals[k, 1, 4, 1].wait_recv()
        whole(k, 7, 1)
        pass_on(k, 0, 0, 0)
        pass_on(k, 1, 0, 1)
        between()
        add_in(k, 0, 0, 0)
        add_in(k, 1, 0, 1)

    returned = {}

    def reduce_end(k, c):
        sums[k, 0, 3, c].wait_recv()
        sums[k, 1, 3, c].wait_recv()
        here = chunk(k, 0, c)
        total = (
            part[k][here, :].astype(f32)
            + rs[k][rs_chunk(k, 0, 3, c), :].astype(f32)
            + rs[k][rs_chunk(k, 1, 3, c), :].astype(f32)
        ).astype(bf16)
        if c == 0:
            ret[k][pl.ds(0, caps[k]), :] = total[: caps[k], :]
        part[k][here, :] = total
        for r in (2 * c, 2 * c + 1):
            if r:
                returned[k, r] = send(
                    part[k].at[pl.ds(r * caps[k], caps[k])],
                    ret[k].at[pl.ds(r * caps[k], caps[k])],
                    ret_send.at[stage[k], r],
                    ret_recv.at[stage[k], r],
                    peers[r],
                )

    m1, m2 = sw1.shape[1] // TILE, sw2.shape[1] // TILE

    def shared_first(source, start, size, target, begin, end):
        def body(i, carry):
            cols = columns(i, TILE)
            value = jnp.dot(
                source[pl.ds(start, size), :], sw1[:, cols], preferred_element_type=f32
            )
            target[:, cols] = jnp.maximum(value + sb1[:, cols], 0.0).astype(bf16)
            return carry

        lax.fori_loop(begin, end, body, 0)

    def shared_second(source, target, start, size, begin, end):
        def body(i, carry):
            cols = columns(i, TILE)
            target[pl.ds(start, size), cols] = jnp.dot(
                source[...], sw2[:, cols], preferred_element_type=f32
            ).astype(bf16)
            return carry

        lax.fori_loop(begin, end, body, 0)

    quarters = 4
    width = sw2.shape[1] // quarters

    def quarter(q):
        return pl.ds(q * width, width)

    def add_crossed(source, cross, target, at, copy, send_sem, recv_sem, q):
        cols = quarter(q)
        copy.wait_recv()
        source[at, cols] = (
            source[at, cols].astype(f32) + cross[:, cols].astype(f32)
        ).astype(bf16)
        return send(source.at[at, cols], target.at[:, cols], send_sem, recv_sem, peers[2])

    def combined(total, own_part, sibling, crossed, cols):
        return (
            total
            + (own_part.astype(f32) + sibling.astype(f32) + crossed.astype(f32))
            + sb2[:, cols]
        )

    half = count // 2

    def block(r, h=None):
        if h is None:
            return pl.ds(r * count, count)
        return pl.ds(r * count + h * half, half)

    def shared_a():
        for c in (1, 2, 3):
            returned["a", c].wait_recv()
        from_sibling, from_y, from_far = [], [], []
        for h in range(2):
            some = pl.ds(h * half, half)
            value = middle[some, :] + jnp.dot(
                back_a[some, :], ret_a[...], preferred_element_type=f32
            )
            middle[some, :] = value
            sgather[some, :] = layer_norm(value, gain2[...]).astype(bf16)
            for r, into in ((2, from_y), (1, from_sibling)):
                into.append(
                    send(
                        sgather.at[some],
                        sgather.at[block(r, h)],
                        sg_send.at[r, h],
                        sg_recv.at[r, h],
                        peers[r],
                    )
                )
        yield
        loads[2].wait()
        loads[3].wait()
        for h in range(2):
            from_sibling[h].wait_recv()
        for q in range(4):
            shared_first(sgather, 0, 2 * count, shidden, q * m1 // 4, (q + 1) * m1 // 4)
            yield
        for q in range(4):
            shared_second(shidden, spart, 0, 2 * count, q * m2 // 4, (q + 1) * m2 // 4)
            yield
        to_own = send(
            spart.at[block(1)], sown, sr_send.at[2, 0], sr_recv.at[2, 0], peers[1]
        )
        yield
        for h in range(2):
            from_y[h].wait_recv()
            from_far.append(
                send(
                    sgather.at[block(2, h)],
                    sgather.at[block(3, h)],
                    sg_send.at[3, h],
                    sg_recv.at[3, h],
                    peers[1],
                )
            )
            yield
        for h in range(2):
            from_far[h].wait_recv()
        for q in range(4):
            shared_first(
                sgather, 2 * count, 2 * count, shidden, q * m1 // 4, (q + 1) * m1 // 4
            )
            yield
        crossed, summed = [], []

        def finish(q):
            summed.append(
                add_crossed(
                    spart, scross, ssum, block(2), crossed[q], sr_send.at[1, q], sr_recv.at[1, q], q
                )
            )

        for q in range(quarters):
            shared_second(
                shidden, spart, 2 * count, 2 * count, q * m2 // 4, (q + 1) * m2 // 4
            )
            crossed.append(
                send(
                    spart.at[block(3), quarter(q)],
                    scross.at[:, quarter(q)],
                    sr_send.at[0, q],
                    sr_recv.at[0, q],
                    peers[1],
                )
            )
            if q:
                finish(q - 1)
            yield
        finish(quarters - 1)
        yield
        to_own.wait_recv()
        for q in range(quarters):
            cols = quarter(q)
            summed[q].wait_recv()
            middle[:, cols] = combined(
                middle[:, cols], spart[block(0), cols], sown[:, cols], ssum[:, cols], cols
            )
            yield

    gather_start("a")
    back_a[...] = jnp.where(
        lax.broadcasted_iota(jnp.int32, (count, 4 * cap_a), 1).astype(f32) == place_column,
        1.0,
        0.0,
    ).astype(bf16)
    middle[...] = tokens[...].astype(f32) + by_group(group_column, group_b2)
    rank_row = column_sum((slot_column >= cap_a) & (i0 < i1))
    rank_row = jnp.where(slot_row >= cap_a, rank_row, -1.0)
    rank_column = row_sum((slot_row >= cap_a) & (i1 < i0))
    rank_column = jnp.where(slot_column >= cap_a, rank_column, -1.0)
    pick = jnp.where(
        lax.broadcasted_iota(jnp.int32, (late, count), 0).astype(f32) == rank_row, 1.0, 0.0
    )
    compact[...] = pick.astype(bf16)
    spread[...] = jnp.where(
        lax.broadcasted_iota(jnp.int32, (count, late), 1).astype(f32) == rank_column, 1.0, 0.0
    ).astype(bf16)
    late_place = jnp.sum(pick * place_row, axis=1, keepdims=True) - 4.0 * cap_a
    late_group = jnp.sum(pick * group_row, axis=1, keepdims=True)
    back_b[...] = jnp.where(
        lax.broadcasted_iota(jnp.int32, (late, 4 * cap_b), 1).astype(f32) == late_place,
        1.0,
        0.0,
    ).astype(bf16)
    middle_b[...] = jnp.dot(
        compact[...], tokens[...], preferred_element_type=f32
    ) + by_group(late_group, group_b2)
    loads[0].wait()
    loads[1].wait()
    for s in (1, 2, 3):
        for c in range(2):
            gather_step("a", s, c)
            for i in (2 * c, 2 * c + 1):
                if s == 1:
                    piece("a", 0, 1, i)
                else:
                    piece("a", 2 * s - 3, 2, i)
    whole("a", 5, 2)
    reduce_start("a", lambda: None)
    drain(8)
    for t in (1, 2):
        for c in order:
            for way in (0, 1):
                add_in("a", way, t, c)

    gather_start("b")
    for c in order:
        reduce_end("a", c)
    shared = shared_a()

    def go_on(pieces=2):
        for _ in range(pieces):
            next(shared, None)

    for s in (1, 2, 3):
        for c in range(2):
            gather_step("b", s, c)
            if s == 3:
                piece("b", 0, 5, 2 * c)
                piece("b", 0, 5, 2 * c + 1)
            go_on()
    whole("b", 5, 2)
    reduce_start("b", lambda: go_on(1))
    for t in (1, 2):
        for c in order:
            for way in (0, 1):
                add_in("b", way, t, c)
            go_on()
    for c in order:
        reduce_end("b", c)
        go_on()

    for c in (1, 2, 3):
        returned["b", c].wait_recv()

    def block_b(r):
        return pl.ds(r * late, late)

    value = middle_b[...] + jnp.dot(back_b[...], ret_b[...], preferred_element_type=f32)
    middle_b[...] = value
    sgather_b[block_b(0), :] = layer_norm(value, gain2[...]).astype(bf16)
    near = {}
    for r in (2, 1):
        near[r] = send(
            sgather_b.at[block_b(0)],
            sgather_b.at[block_b(r)],
            sg_send.at[r, 2],
            sg_recv.at[r, 2],
            peers[r],
        )
    for _ in shared:
        pass
    drain(16)
    near[2].wait_recv()
    near[3] = send(
        sgather_b.at[block_b(2)],
        sgather_b.at[block_b(3)],
        sg_send.at[3, 2],
        sg_recv.at[3, 2],
        peers[1],
    )
    near[1].wait_recv()
    near[3].wait_recv()
    shared_first(sgather_b, 0, 4 * late, shidden_b, 0, m1)
    crossed, to_own, summed = [], [], []

    def finish_b(q):
        summed.append(
            add_crossed(
                spart_b,
                scross_b,
                ssum_b,
                block_b(2),
                crossed[q],
                sr_send.at[4, q],
                sr_recv.at[4, q],
                q,
            )
        )

    for q in range(quarters):
        cols = quarter(q)
        shared_second(shidden_b, spart_b, 0, 4 * late, q * m2 // 4, (q + 1) * m2 // 4)
        crossed.append(
            send(
                spart_b.at[block_b(3), cols],
                scross_b.at[:, cols],
                sr_send.at[3, q],
                sr_recv.at[3, q],
                peers[1],
            )
        )
        to_own.append(
            send(
                spart_b.at[block_b(1), cols],
                sown_b.at[:, cols],
                sr_send.at[5, q],
                sr_recv.at[5, q],
                peers[1],
            )
        )
        if q:
            finish_b(q - 1)
    finish_b(quarters - 1)
    for q in range(quarters):
        cols = quarter(q)
        to_own[q].wait_recv()
        summed[q].wait_recv()
        late_out = combined(
            middle_b[:, cols], spart_b[block_b(0), cols], sown_b[:, cols], ssum_b[:, cols], cols
        ).astype(bf16)
        placed = jnp.dot(spread[...], late_out, preferred_element_type=f32)
        is_late = jnp.sum(spread[...].astype(f32), axis=1, keepdims=True)
        encoded[:, cols] = jnp.where(is_late > 0.5, placed, middle[:, cols]).astype(bf16)
    drain(0)


def fused_on_device(
    tokens,
    languages,
    lang_group,
    group_gain,
    group_w1,
    group_b1,
    group_w2,
    group_b2,
    shared_gain,
    shared_w1,
    shared_b1,
    shared_w2,
    shared_b2,
):
    count, width = tokens.shape
    unit = group_w1.shape[2]
    shared_unit = shared_w1.shape[1]
    cap_a, cap_b = count // 4, count // 8
    late = count // 4
    bf16, f32 = jnp.bfloat16, jnp.float32
    in_vmem = pl.BlockSpec(memory_space=pltpu.VMEM)
    anywhere = pl.BlockSpec(memory_space=pl.ANY)
    dma = pltpu.SemaphoreType.DMA

    def held(rows, columns=width, dtype=bf16):
        return pltpu.VMEM((rows, columns), dtype)

    return pl.pallas_call(
        fused_kernel,
        out_shape=jax.ShapeDtypeStruct((count, width), bf16),
        in_specs=[in_vmem] * 9 + [anywhere] * 4,
        out_specs=in_vmem,
        scratch_shapes=[
            held(width, unit),
            held(unit),
            held(width, shared_unit),
            held(shared_unit),
            held(4 * (cap_a + cap_b)),
            held(32 * cap_a),
            held(32 * cap_a),
            held(28 * cap_a),
            held(4 * cap_a),
            held(32 * cap_b),
            held(32 * cap_b),
            held(28 * cap_b),
            held(4 * cap_b),
            held(max(8 * cap_a, 20 * cap_b), unit),
            held(4 * count),
            held(2 * count, shared_unit),
            held(4 * count),
            held(count),
            held(count),
            held(count),
            held(count, dtype=f32),
            held(4 * late),
            held(4 * late, shared_unit),
            held(4 * late),
            held(late),
            held(late),
            held(late),
            held(late, dtype=f32),
            held(count, 4 * cap_a),
            held(late, 4 * cap_b),
            held(late, count),
            held(count, late),
            dma((4,)),
            dma((2,)),
            dma((2, 4)),
            dma((2, 4)),
            dma((2, 2, 4, 2)),
            dma((2, 2, 5, 2)),
            dma((2, 2, 4, 2)),
            dma((2, 2, 4, 2)),
            dma((2, 4)),
            dma((2, 4)),
            dma((4, 3)),
            dma((4, 3)),
            dma((6, 4)),
            dma((6, 4)),
        ],
        compiler_params=pltpu.CompilerParams(
            collective_id=0, has_side_effects=True, vmem_limit_bytes=62 * 1024 * 1024
        ),
    )(
        tokens,
        languages[None, :],
        lang_group[None, :],
        group_gain,
        group_b2,
        group_b1,
        shared_gain[None, :],
        shared_b1[None, :],
        shared_b2[None, :],
        group_w1[0],
        group_w2[0],
        shared_w1,
        shared_w2,
    )


def plain_on_device(
    tokens,
    languages,
    lang_group,
    group_gain,
    group_w1,
    group_b1,
    group_w2,
    group_b2,
    shared_gain,
    shared_w1,
    shared_b1,
    shared_w2,
    shared_b2,
):
    tok_dev = tokens.shape[0]
    width_model = tokens.shape[1]
    num_groups = group_gain.shape[0]
    num_langs = lang_group.shape[0]
    capacity = 3 * tok_dev // (2 * lax.axis_size("group"))
    residual_in = tokens.astype(jnp.float32)
    lang_hit = (languages[:, None] == jnp.arange(num_langs, dtype=jnp.int32)[None, :]).astype(
        jnp.int32
    )
    group_of = jnp.sum(lang_hit * lang_group[None, :], axis=1)
    onehot = (group_of[:, None] == jnp.arange(num_groups, dtype=jnp.int32)[None, :]).astype(
        jnp.int32
    )
    earlier = jnp.cumsum(onehot, axis=0) - onehot
    slot_index = jnp.sum(earlier * onehot, axis=1)
    position = group_of * capacity + slot_index
    dispatch_map = (
        position[None, :] == jnp.arange(num_groups * capacity, dtype=jnp.int32)[:, None]
    ).astype(jnp.bfloat16)
    onehot_float = onehot.astype(jnp.float32)
    row_gains = jnp.dot(onehot_float, group_gain, precision=lax.Precision.HIGHEST)
    normed = layer_norm(residual_in, row_gains).astype(jnp.bfloat16)
    outgoing = jnp.dot(dispatch_map, normed, preferred_element_type=jnp.float32).astype(
        jnp.bfloat16
    )
    outgoing = outgoing.reshape(num_groups, capacity, width_model)
    arrived = lax.all_to_all(outgoing, "group", split_axis=0, concat_axis=0, tiled=True)
    group_rows = arrived.reshape(num_groups * capacity, width_model)
    first_proj = group_w1[0]
    first_bias = group_b1[0]
    second_proj = group_w2[0]
    hidden = jax.nn.relu(
        jnp.dot(
            lax.all_gather(group_rows, "within", axis=0, tiled=True),
            first_proj,
            preferred_element_type=jnp.float32,
        )
        + first_bias
    ).astype(jnp.bfloat16)
    selected = hidden
    summed = lax.psum_scatter(
        jnp.dot(selected, second_proj, preferred_element_type=jnp.float32).astype(jnp.bfloat16),
        "within",
        scatter_dimension=0,
        tiled=True,
    )
    returned = lax.all_to_all(
        summed.reshape(num_groups, capacity, width_model),
        "group",
        split_axis=0,
        concat_axis=0,
        tiled=True,
    )
    returned = returned.reshape(num_groups * capacity, width_model)
    group_out = lax.dot_general(
        dispatch_map, returned, (((0,), (0,)), ((), ())), preferred_element_type=jnp.float32
    )
    group_bias = jnp.dot(onehot_float, group_b2, precision=lax.Precision.HIGHEST)
    middle = residual_in + group_out + group_bias
    shared_in = layer_norm(middle, shared_gain).astype(jnp.bfloat16)
    shared_hidden = jax.nn.relu(
        jnp.dot(
            lax.all_gather(shared_in, "group", axis=0, tiled=True),
            shared_w1,
            preferred_element_type=jnp.float32,
        )
        + shared_b1
    ).astype(jnp.bfloat16)
    selected = shared_hidden
    shared_out = lax.psum_scatter(
        jnp.dot(selected, shared_w2, preferred_element_type=jnp.float32).astype(jnp.bfloat16),
        "group",
        scatter_dimension=0,
        tiled=True,
    ).astype(jnp.float32)
    return (middle + shared_out + shared_b2).astype(jnp.bfloat16)


def solution(mesh):
    placed = (
        P(("group", "within"), None),
        P(("group", "within")),
        P(),
        P(),
        P("group", None, "within"),
        P("group", "within"),
        P("group", "within", None),
        P(),
        P(),
        P(None, "group"),
        P("group"),
        P("group", None),
        P(),
    )
    fits = mesh.shape["group"] == 4 and mesh.shape["within"] == 8
    return jax.shard_map(
        fused_on_device if fits else plain_on_device,
        mesh=mesh,
        in_specs=placed,
        out_specs=P(("group", "within"), None),
        check_vma=False,
    )
```

```python
import jax
import jax.numpy as jnp
from jax import lax
from jax.experimental import pallas as pl
from jax.experimental.pallas import tpu as pltpu
from jax.sharding import PartitionSpec as P

MESH = pl.DeviceIdType.MESH
TILE = 512


def layer_norm(values, gains):
    centre = jnp.mean(values, axis=-1, keepdims=True)
    centred = values - centre
    spread = jnp.mean(centred * centred, axis=-1, keepdims=True)
    return centred * lax.rsqrt(spread + 1e-05) * gains


def columns(tile, size):
    return pl.ds(pl.multiple_of(tile * size, size), size)


def row_sum(mask):
    return jnp.sum(jnp.where(mask, 1.0, 0.0), axis=1, keepdims=True)


def column_sum(mask):
    return jnp.sum(jnp.where(mask, 1.0, 0.0), axis=0, keepdims=True)


def by_group(column, table):
    value = jnp.where(column == 0.0, table[0:1, :], 0.0)
    for i in range(1, table.shape[0]):
        value = jnp.where(column == float(i), table[i : i + 1, :], value)
    return value


def fused_kernel(
    tokens,
    languages,
    lang_group,
    group_gain,
    group_b2,
    b1,
    gain2,
    sb1,
    sb2,
    w1_hbm,
    w2_hbm,
    sw1_hbm,
    sw2_hbm,
    encoded,
    w1,
    w2,
    sw1,
    sw2,
    outgoing,
    rows_a,
    part_a,
    rs_a,
    ret_a,
    rows_b,
    part_b,
    rs_b,
    ret_b,
    hidden,
    sgather,
    shidden,
    spart,
    sown,
    scross,
    ssum,
    middle,
    sgather_b,
    shidden_b,
    spart_b,
    sown_b,
    scross_b,
    ssum_b,
    middle_b,
    back_a,
    back_b,
    compact,
    spread,
    w_sem,
    local_sem,
    disp_send,
    disp_recv,
    g_send,
    g_recv,
    r_send,
    r_recv,
    ret_send,
    ret_recv,
    sg_send,
    sg_recv,
    sr_send,
    sr_recv,
):
    bf16, f32 = jnp.bfloat16, jnp.float32
    g = lax.axis_index("group")
    w = lax.axis_index("within")
    x, z = lax.rem(w, 2), lax.div(w, 2)
    p = z + x * (7 - 2 * z)

    def device_at(q):
        q = lax.rem(q + 8, 8)
        far = lax.div(q, 4)
        return 2 * q + far * (15 - 4 * q)

    right = (g, device_at(p + 1))
    left = (g, device_at(p - 1))
    yy, core = lax.div(g, 2), lax.rem(g, 2)
    peers = [
        None,
        (2 * yy + 1 - core, w),
        (2 * (1 - yy) + core, w),
        (2 * (1 - yy) + 1 - core, w),
    ]
    barrier = pltpu.get_barrier_semaphore()
    for device in (right, left, peers[1], peers[2], peers[3]):
        pl.semaphore_signal(barrier, inc=1, device_id=device, device_id_type=MESH)

    loads = []
    for i, (src, dst) in enumerate(
        ((w1_hbm, w1), (w2_hbm, w2), (sw1_hbm, sw1), (sw2_hbm, sw2))
    ):
        copy = pltpu.make_async_copy(src, dst, w_sem.at[i])
        copy.start()
        loads.append(copy)

    count = tokens.shape[0]
    cap_a, cap_b = count // 4, count // 8
    late = count // 4
    i0 = lax.broadcasted_iota(jnp.int32, (count, count), 0)
    i1 = lax.broadcasted_iota(jnp.int32, (count, count), 1)
    eye = i0 == i1

    def to_column(row):
        return jnp.sum(jnp.where(eye, row, 0.0), axis=1, keepdims=True)

    def to_row(column):
        return jnp.sum(jnp.where(eye, column, 0.0), axis=0, keepdims=True)

    num_langs = lang_group.shape[1]
    lang = to_column(languages[...].astype(f32))
    lang_ids = lax.broadcasted_iota(jnp.int32, (count, num_langs), 1).astype(f32)
    group_column = jnp.sum(
        jnp.where(lang == lang_ids, lang_group[...].astype(f32), 0.0), axis=1, keepdims=True
    )
    group_row = to_row(group_column)
    same = group_column == group_row
    slot_column = row_sum(same & (i1 < i0))
    slot_row = column_sum(same & (i0 < i1))
    my_y, my_core = yy.astype(f32), core.astype(f32)

    def position(group, slot):
        gy = jnp.where(group >= 2.0, 1.0, 0.0)
        dy, dc = gy - my_y, group - 2.0 * gy - my_core
        r = 2.0 * dy * dy + dc * dc
        return jnp.where(
            slot < cap_a, r * cap_a + slot, count + r * cap_b + slot - cap_a
        )

    place_column = position(group_column, slot_column)
    place_row = position(group_row, slot_row)
    total_slots = 4 * (cap_a + cap_b)
    out_map = (
        lax.broadcasted_iota(jnp.int32, (total_slots, count), 0).astype(f32) == place_row
    )
    normed = layer_norm(
        tokens[...].astype(f32), by_group(group_column, group_gain)
    ).astype(bf16)
    outgoing[...] = jnp.dot(
        jnp.where(out_map, 1.0, 0.0).astype(bf16), normed, preferred_element_type=f32
    ).astype(bf16)
    base = {"a": 0, "b": 4 * cap_a}
    caps = {"a": cap_a, "b": cap_b}
    stage = {"a": 0, "b": 1}
    rows = {"a": rows_a, "b": rows_b}
    part = {"a": part_a, "b": part_b}
    rs = {"a": rs_a, "b": rs_b}
    ret = {"a": ret_a, "b": ret_b}
    own = {}
    for k in "ab":
        own[k] = pltpu.make_async_copy(
            outgoing.at[pl.ds(base[k], caps[k])],
            rows[k].at[pl.ds(0, caps[k])],
            local_sem.at[stage[k]],
        )
        own[k].start()
    pl.semaphore_wait(barrier, 5)

    pending = []

    def send(src, dst, send_sem, recv_sem, device):
        copy = pltpu.make_async_remote_copy(
            src_ref=src,
            dst_ref=dst,
            send_sem=send_sem,
            recv_sem=recv_sem,
            device_id=device,
            device_id_type=MESH,
        )
        copy.start()
        pending.append(copy)
        return copy

    def drain(keep):
        while len(pending) > keep:
            pending.pop(0).wait_send()

    def chunk(k, slot, c):
        return pl.ds((slot * 4 + 2 * c) * caps[k], 2 * caps[k])

    dispatch = {}
    for k in "ab":
        for r in (2, 3, 1):
            dispatch[k, r] = send(
                outgoing.at[pl.ds(base[k] + r * caps[k], caps[k])],
                rows[k].at[pl.ds(r * caps[k], caps[k])],
                disp_send.at[stage[k], r],
                disp_recv.at[stage[k], r],
                peers[r],
            )

    def slot_of(way, s):
        return 7 if s == 4 else (0 if s == 0 else 2 * s - 1 + way)

    arrivals = {}

    def forward(k, way, s, c):
        arrivals[k, way, s + 1, c] = send(
            rows[k].at[chunk(k, slot_of(way, s), c)],
            rows[k].at[chunk(k, slot_of(way, s + 1), c)],
            g_send.at[stage[k], way, s, c],
            g_recv.at[stage[k], way, s + 1, c],
            right if way == 0 else left,
        )

    def first_tiles(k, slot, slots, begin, end):
        size = slots * 4 * caps[k]

        def body(i, carry):
            cols = columns(i, TILE)
            value = jnp.dot(
                rows[k][pl.ds(slot * 4 * caps[k], size), :],
                w1[:, cols],
                preferred_element_type=f32,
            )
            hidden[pl.ds(0, size), cols] = jnp.maximum(value + b1[:, cols], 0.0).astype(bf16)
            return carry

        lax.fori_loop(begin, end, body, 0)

    def second_tiles(k, slot, slots, begin, end):
        size = slots * 4 * caps[k]

        def body(i, carry):
            cols = columns(i, TILE)
            part[k][pl.ds(slot * 4 * caps[k], size), cols] = jnp.dot(
                hidden[pl.ds(0, size), :], w2[:, cols], preferred_element_type=f32
            ).astype(bf16)
            return carry

        lax.fori_loop(begin, end, body, 0)

    n1, n2 = w1.shape[1] // TILE, w2.shape[1] // TILE

    def piece(k, slot, slots, c):
        if c < 2:
            first_tiles(k, slot, slots, c * n1 // 2, (c + 1) * n1 // 2)
        else:
            second_tiles(k, slot, slots, (c - 2) * n2 // 2, (c - 1) * n2 // 2)

    def whole(k, slot, slots):
        first_tiles(k, slot, slots, 0, n1)
        second_tiles(k, slot, slots, 0, n2)

    def gather_start(k):
        own[k].wait()
        for c in range(2):
            for r in (2 * c, 2 * c + 1):
                if r:
                    dispatch[k, r].wait_recv()
            forward(k, 0, 0, c)
            forward(k, 1, 0, c)

    def gather_step(k, s, c):
        for way in (0, 1):
            arrivals[k, way, s, c].wait_recv()
            if s < 3 or c == way:
                forward(k, way, s, c)

    def rs_slot(way, t):
        return (7, 6 - way, 4 - way, 2 - way)[t]

    def rs_chunk(k, way, t, c):
        at = way * 14 + (0 if t == 0 else 4 * t - 2 + 2 * c)
        return pl.ds(at * caps[k], 2 * caps[k])

    sums = {}

    def pass_on(k, way, t, c):
        sums[k, way, t, c] = send(
            part[k].at[chunk(k, rs_slot(way, t), c)],
            rs[k].at[rs_chunk(k, way, t, c)],
            r_send.at[stage[k], way, t, c],
            r_recv.at[stage[k], way, t, c],
            right if way == 0 else left,
        )

    def add_in(k, way, t, c):
        sums[k, way, t, c].wait_recv()
        here = chunk(k, rs_slot(way, t + 1), c)
        part[k][here, :] = (
            part[k][here, :].astype(f32) + rs[k][rs_chunk(k, way, t, c), :].astype(f32)
        ).astype(bf16)
        pass_on(k, way, t + 1, c)

    order = (1, 0)

    def reduce_start(k, between):
        pass_on(k, 0, 1, 1)
        pass_on(k, 1, 1, 0)
        between()
        arrivals[k, 0, 4, 0].wait_recv()
        arrivals[k, 1, 4, 1].wait_recv()
        whole(k, 7, 1)
        pass_on(k, 0, 0, 0)
        pass_on(k, 1, 0, 1)
        between()

    def reduce_alternating(k):
        for t in (0, 1):
            for way in (0, 1):
                add_in(k, way, t + 1, 1 - way)
            for way in (0, 1):
                add_in(k, way, t, way)
        for way in (0, 1):
            add_in(k, way, 2, way)

    returned = {}

    def reduce_end(k, c):
        sums[k, 0, 3, c].wait_recv()
        sums[k, 1, 3, c].wait_recv()
        here = chunk(k, 0, c)
        total = (
            part[k][here, :].astype(f32)
            + rs[k][rs_chunk(k, 0, 3, c), :].astype(f32)
            + rs[k][rs_chunk(k, 1, 3, c), :].astype(f32)
        ).astype(bf16)
        if c == 0:
            ret[k][pl.ds(0, caps[k]), :] = total[: caps[k], :]
        part[k][here, :] = total
        for r in (2 * c, 2 * c + 1):
            if r:
                returned[k, r] = send(
                    part[k].at[pl.ds(r * caps[k], caps[k])],
                    ret[k].at[pl.ds(r * caps[k], caps[k])],
                    ret_send.at[stage[k], r],
                    ret_recv.at[stage[k], r],
                    peers[r],
                )

    m1, m2 = sw1.shape[1] // TILE, sw2.shape[1] // TILE

    def shared_first(source, start, size, target, begin, end):
        def body(i, carry):
            cols = columns(i, TILE)
            value = jnp.dot(
                source[pl.ds(start, size), :], sw1[:, cols], preferred_element_type=f32
            )
            target[:, cols] = jnp.maximum(value + sb1[:, cols], 0.0).astype(bf16)
            return carry

        lax.fori_loop(begin, end, body, 0)

    def shared_second(source, target, start, size, begin, end):
        def body(i, carry):
            cols = columns(i, TILE)
            target[pl.ds(start, size), cols] = jnp.dot(
                source[...], sw2[:, cols], preferred_element_type=f32
            ).astype(bf16)
            return carry

        lax.fori_loop(begin, end, body, 0)

    quarters = 4
    width = sw2.shape[1] // quarters

    def quarter(q):
        return pl.ds(q * width, width)

    def add_crossed(source, cross, target, at, copy, send_sem, recv_sem, q):
        cols = quarter(q)
        copy.wait_recv()
        source[at, cols] = (
            source[at, cols].astype(f32) + cross[:, cols].astype(f32)
        ).astype(bf16)
        return send(source.at[at, cols], target.at[:, cols], send_sem, recv_sem, peers[2])

    def combined(total, own_part, sibling, crossed, cols):
        return (
            total
            + (own_part.astype(f32) + sibling.astype(f32) + crossed.astype(f32))
            + sb2[:, cols]
        )

    half = count // 2

    def block(r, h=None):
        if h is None:
            return pl.ds(r * count, count)
        return pl.ds(r * count + h * half, half)

    def shared_a():
        for c in (1, 2, 3):
            returned["a", c].wait_recv()
        from_sibling, from_y, from_far = [], [], []
        for h in range(2):
            some = pl.ds(h * half, half)
            value = middle[some, :] + jnp.dot(
                back_a[some, :], ret_a[...], preferred_element_type=f32
            )
            middle[some, :] = value
            sgather[some, :] = layer_norm(value, gain2[...]).astype(bf16)
            for r, into in ((2, from_y), (1, from_sibling)):
                into.append(
                    send(
                        sgather.at[some],
                        sgather.at[block(r, h)],
                        sg_send.at[r, h],
                        sg_recv.at[r, h],
                        peers[r],
                    )
                )
        yield
        loads[2].wait()
        loads[3].wait()
        for h in range(2):
            from_sibling[h].wait_recv()
        for q in range(4):
            shared_first(sgather, 0, 2 * count, shidden, q * m1 // 4, (q + 1) * m1 // 4)
            yield
        for q in range(4):
            shared_second(shidden, spart, 0, 2 * count, q * m2 // 4, (q + 1) * m2 // 4)
            yield
        to_own = send(
            spart.at[block(1)], sown, sr_send.at[2, 0], sr_recv.at[2, 0], peers[1]
        )
        yield
        for h in range(2):
            from_y[h].wait_recv()
            from_far.append(
                send(
                    sgather.at[block(2, h)],
                    sgather.at[block(3, h)],
                    sg_send.at[3, h],
                    sg_recv.at[3, h],
                    peers[1],
                )
            )
            yield
        for h in range(2):
            from_far[h].wait_recv()
        for q in range(4):
            shared_first(
                sgather, 2 * count, 2 * count, shidden, q * m1 // 4, (q + 1) * m1 // 4
            )
            yield
        crossed, summed = [], []

        def finish(q):
            summed.append(
                add_crossed(
                    spart, scross, ssum, block(2), crossed[q], sr_send.at[1, q], sr_recv.at[1, q], q
                )
            )

        for q in range(quarters):
            shared_second(
                shidden, spart, 2 * count, 2 * count, q * m2 // 4, (q + 1) * m2 // 4
            )
            crossed.append(
                send(
                    spart.at[block(3), quarter(q)],
                    scross.at[:, quarter(q)],
                    sr_send.at[0, q],
                    sr_recv.at[0, q],
                    peers[1],
                )
            )
            if q:
                finish(q - 1)
            yield
        finish(quarters - 1)
        yield
        to_own.wait_recv()
        for q in range(quarters):
            cols = quarter(q)
            summed[q].wait_recv()
            middle[:, cols] = combined(
                middle[:, cols], spart[block(0), cols], sown[:, cols], ssum[:, cols], cols
            )
            yield

    gather_start("a")
    back_a[...] = jnp.where(
        lax.broadcasted_iota(jnp.int32, (count, 4 * cap_a), 1).astype(f32) == place_column,
        1.0,
        0.0,
    ).astype(bf16)
    middle[...] = tokens[...].astype(f32) + by_group(group_column, group_b2)
    rank_row = column_sum((slot_column >= cap_a) & (i0 < i1))
    rank_row = jnp.where(slot_row >= cap_a, rank_row, -1.0)
    rank_column = row_sum((slot_row >= cap_a) & (i1 < i0))
    rank_column = jnp.where(slot_column >= cap_a, rank_column, -1.0)
    pick = jnp.where(
        lax.broadcasted_iota(jnp.int32, (late, count), 0).astype(f32) == rank_row, 1.0, 0.0
    )
    compact[...] = pick.astype(bf16)
    spread[...] = jnp.where(
        lax.broadcasted_iota(jnp.int32, (count, late), 1).astype(f32) == rank_column, 1.0, 0.0
    ).astype(bf16)
    late_place = jnp.sum(pick * place_row, axis=1, keepdims=True) - 4.0 * cap_a
    late_group = jnp.sum(pick * group_row, axis=1, keepdims=True)
    back_b[...] = jnp.where(
        lax.broadcasted_iota(jnp.int32, (late, 4 * cap_b), 1).astype(f32) == late_place,
        1.0,
        0.0,
    ).astype(bf16)
    middle_b[...] = jnp.dot(
        compact[...], tokens[...], preferred_element_type=f32
    ) + by_group(late_group, group_b2)
    loads[0].wait()
    loads[1].wait()
    for s in (1, 2, 3):
        for c in range(2):
            gather_step("a", s, c)
            for i in (2 * c, 2 * c + 1):
                if s == 1:
                    piece("a", 0, 1, i)
                else:
                    piece("a", 2 * s - 3, 2, i)
    whole("a", 5, 2)
    reduce_start("a", lambda: None)
    drain(8)
    reduce_alternating("a")

    gather_start("b")
    for c in order:
        reduce_end("a", c)
    shared = shared_a()

    def go_on(pieces=2):
        for _ in range(pieces):
            next(shared, None)

    for s in (1, 2, 3):
        for c in range(2):
            gather_step("b", s, c)
            if s == 3:
                piece("b", 0, 5, 2 * c)
                piece("b", 0, 5, 2 * c + 1)
            go_on()
    whole("b", 5, 2)
    reduce_start("b", lambda: go_on(1))
    add_in("b", 0, 0, 0)
    add_in("b", 1, 0, 1)
    for t in (1, 2):
        for c in order:
            for way in (0, 1):
                add_in("b", way, t, c)
            go_on()
    for c in order:
        reduce_end("b", c)
        go_on()

    for c in (1, 2, 3):
        returned["b", c].wait_recv()

    def block_b(r):
        return pl.ds(r * late, late)

    value = middle_b[...] + jnp.dot(back_b[...], ret_b[...], preferred_element_type=f32)
    middle_b[...] = value
    sgather_b[block_b(0), :] = layer_norm(value, gain2[...]).astype(bf16)
    near = {}
    for r in (2, 1):
        near[r] = send(
            sgather_b.at[block_b(0)],
            sgather_b.at[block_b(r)],
            sg_send.at[r, 2],
            sg_recv.at[r, 2],
            peers[r],
        )
    for _ in shared:
        pass
    drain(16)
    near[2].wait_recv()
    near[3] = send(
        sgather_b.at[block_b(2)],
        sgather_b.at[block_b(3)],
        sg_send.at[3, 2],
        sg_recv.at[3, 2],
        peers[1],
    )
    near[1].wait_recv()
    near[3].wait_recv()
    shared_first(sgather_b, 0, 4 * late, shidden_b, 0, m1)
    crossed, to_own, summed = [], [], []

    def finish_b(q):
        summed.append(
            add_crossed(
                spart_b,
                scross_b,
                ssum_b,
                block_b(2),
                crossed[q],
                sr_send.at[4, q],
                sr_recv.at[4, q],
                q,
            )
        )

    for q in range(quarters):
        cols = quarter(q)
        shared_second(shidden_b, spart_b, 0, 4 * late, q * m2 // 4, (q + 1) * m2 // 4)
        crossed.append(
            send(
                spart_b.at[block_b(3), cols],
                scross_b.at[:, cols],
                sr_send.at[3, q],
                sr_recv.at[3, q],
                peers[1],
            )
        )
        to_own.append(
            send(
                spart_b.at[block_b(1), cols],
                sown_b.at[:, cols],
                sr_send.at[5, q],
                sr_recv.at[5, q],
                peers[1],
            )
        )
        if q:
            finish_b(q - 1)
    finish_b(quarters - 1)
    is_late = jnp.sum(spread[...].astype(f32), axis=1, keepdims=True)
    for q in range(quarters):
        cols = quarter(q)
        to_own[q].wait_recv()
        summed[q].wait_recv()
        late_out = combined(
            middle_b[:, cols], spart_b[block_b(0), cols], sown_b[:, cols], ssum_b[:, cols], cols
        ).astype(bf16)
        placed = jnp.dot(spread[...], late_out, preferred_element_type=f32)
        encoded[:, cols] = jnp.where(is_late > 0.5, placed, middle[:, cols])
    drain(0)


def fused_on_device(
    tokens,
    languages,
    lang_group,
    group_gain,
    group_w1,
    group_b1,
    group_w2,
    group_b2,
    shared_gain,
    shared_w1,
    shared_b1,
    shared_w2,
    shared_b2,
):
    count, width = tokens.shape
    unit = group_w1.shape[2]
    shared_unit = shared_w1.shape[1]
    cap_a, cap_b = count // 4, count // 8
    late = count // 4
    bf16, f32 = jnp.bfloat16, jnp.float32
    in_vmem = pl.BlockSpec(memory_space=pltpu.VMEM)
    anywhere = pl.BlockSpec(memory_space=pl.ANY)
    dma = pltpu.SemaphoreType.DMA

    def held(rows, columns=width, dtype=bf16):
        return pltpu.VMEM((rows, columns), dtype)

    return pl.pallas_call(
        fused_kernel,
        out_shape=jax.ShapeDtypeStruct((count, width), f32),
        in_specs=[in_vmem] * 9 + [anywhere] * 4,
        out_specs=in_vmem,
        scratch_shapes=[
            held(width, unit),
            held(unit),
            held(width, shared_unit),
            held(shared_unit),
            held(4 * (cap_a + cap_b)),
            held(32 * cap_a),
            held(32 * cap_a),
            held(28 * cap_a),
            held(4 * cap_a),
            held(32 * cap_b),
            held(32 * cap_b),
            held(28 * cap_b),
            held(4 * cap_b),
            held(max(8 * cap_a, 20 * cap_b), unit),
            held(4 * count),
            held(2 * count, shared_unit),
            held(4 * count),
            held(count),
            held(count),
            held(count),
            held(count, dtype=f32),
            held(4 * late),
            held(4 * late, shared_unit),
            held(4 * late),
            held(late),
            held(late),
            held(late),
            held(late, dtype=f32),
            held(count, 4 * cap_a),
            held(late, 4 * cap_b),
            held(late, count),
            held(count, late),
            dma((4,)),
            dma((2,)),
            dma((2, 4)),
            dma((2, 4)),
            dma((2, 2, 4, 2)),
            dma((2, 2, 5, 2)),
            dma((2, 2, 4, 2)),
            dma((2, 2, 4, 2)),
            dma((2, 4)),
            dma((2, 4)),
            dma((4, 3)),
            dma((4, 3)),
            dma((6, 4)),
            dma((6, 4)),
        ],
        compiler_params=pltpu.CompilerParams(
            collective_id=0, has_side_effects=True, vmem_limit_bytes=62 * 1024 * 1024
        ),
    )(
        tokens,
        languages[None, :],
        lang_group[None, :],
        group_gain,
        group_b2,
        group_b1,
        shared_gain[None, :],
        shared_b1[None, :],
        shared_b2[None, :],
        group_w1[0],
        group_w2[0],
        shared_w1,
        shared_w2,
    ).astype(bf16)


def plain_on_device(
    tokens,
    languages,
    lang_group,
    group_gain,
    group_w1,
    group_b1,
    group_w2,
    group_b2,
    shared_gain,
    shared_w1,
    shared_b1,
    shared_w2,
    shared_b2,
):
    tok_dev = tokens.shape[0]
    width_model = tokens.shape[1]
    num_groups = group_gain.shape[0]
    num_langs = lang_group.shape[0]
    capacity = 3 * tok_dev // (2 * lax.axis_size("group"))
    residual_in = tokens.astype(jnp.float32)
    lang_hit = (languages[:, None] == jnp.arange(num_langs, dtype=jnp.int32)[None, :]).astype(
        jnp.int32
    )
    group_of = jnp.sum(lang_hit * lang_group[None, :], axis=1)
    onehot = (group_of[:, None] == jnp.arange(num_groups, dtype=jnp.int32)[None, :]).astype(
        jnp.int32
    )
    earlier = jnp.cumsum(onehot, axis=0) - onehot
    slot_index = jnp.sum(earlier * onehot, axis=1)
    position = group_of * capacity + slot_index
    dispatch_map = (
        position[None, :] == jnp.arange(num_groups * capacity, dtype=jnp.int32)[:, None]
    ).astype(jnp.bfloat16)
    onehot_float = onehot.astype(jnp.float32)
    row_gains = jnp.dot(onehot_float, group_gain, precision=lax.Precision.HIGHEST)
    normed = layer_norm(residual_in, row_gains).astype(jnp.bfloat16)
    outgoing = jnp.dot(dispatch_map, normed, preferred_element_type=jnp.float32).astype(
        jnp.bfloat16
    )
    outgoing = outgoing.reshape(num_groups, capacity, width_model)
    arrived = lax.all_to_all(outgoing, "group", split_axis=0, concat_axis=0, tiled=True)
    group_rows = arrived.reshape(num_groups * capacity, width_model)
    first_proj = group_w1[0]
    first_bias = group_b1[0]
    second_proj = group_w2[0]
    hidden = jax.nn.relu(
        jnp.dot(
            lax.all_gather(group_rows, "within", axis=0, tiled=True),
            first_proj,
            preferred_element_type=jnp.float32,
        )
        + first_bias
    ).astype(jnp.bfloat16)
    selected = hidden
    summed = lax.psum_scatter(
        jnp.dot(selected, second_proj, preferred_element_type=jnp.float32).astype(jnp.bfloat16),
        "within",
        scatter_dimension=0,
        tiled=True,
    )
    returned = lax.all_to_all(
        summed.reshape(num_groups, capacity, width_model),
        "group",
        split_axis=0,
        concat_axis=0,
        tiled=True,
    )
    returned = returned.reshape(num_groups * capacity, width_model)
    group_out = lax.dot_general(
        dispatch_map, returned, (((0,), (0,)), ((), ())), preferred_element_type=jnp.float32
    )
    group_bias = jnp.dot(onehot_float, group_b2, precision=lax.Precision.HIGHEST)
    middle = residual_in + group_out + group_bias
    shared_in = layer_norm(middle, shared_gain).astype(jnp.bfloat16)
    shared_hidden = jax.nn.relu(
        jnp.dot(
            lax.all_gather(shared_in, "group", axis=0, tiled=True),
            shared_w1,
            preferred_element_type=jnp.float32,
        )
        + shared_b1
    ).astype(jnp.bfloat16)
    selected = shared_hidden
    shared_out = lax.psum_scatter(
        jnp.dot(selected, shared_w2, preferred_element_type=jnp.float32).astype(jnp.bfloat16),
        "group",
        scatter_dimension=0,
        tiled=True,
    ).astype(jnp.float32)
    return (middle + shared_out + shared_b2).astype(jnp.bfloat16)


def solution(mesh):
    placed = (
        P(("group", "within"), None),
        P(("group", "within")),
        P(),
        P(),
        P("group", None, "within"),
        P("group", "within"),
        P("group", "within", None),
        P(),
        P(),
        P(None, "group"),
        P("group"),
        P("group", None),
        P(),
    )
    fits = mesh.shape["group"] == 4 and mesh.shape["within"] == 8
    return jax.shard_map(
        fused_on_device if fits else plain_on_device,
        mesh=mesh,
        in_specs=placed,
        out_specs=P(("group", "within"), None),
        check_vma=False,
    )
```

```python
import jax
import jax.numpy as jnp
from jax import lax
from jax.experimental import pallas as pl
from jax.experimental.pallas import tpu as pltpu
from jax.sharding import PartitionSpec as P

MESH = pl.DeviceIdType.MESH
TILE = 256


def layer_norm(values, gains):
    centre = jnp.mean(values, axis=-1, keepdims=True)
    centred = values - centre
    spread = jnp.mean(centred * centred, axis=-1, keepdims=True)
    return centred * lax.rsqrt(spread + 1e-05) * gains


def columns(tile, size):
    return pl.ds(pl.multiple_of(tile * size, size), size)


def row_sum(mask):
    return jnp.sum(jnp.where(mask, 1.0, 0.0), axis=1, keepdims=True)


def column_sum(mask):
    return jnp.sum(jnp.where(mask, 1.0, 0.0), axis=0, keepdims=True)


def by_group(column, table):
    value = jnp.where(column == 0.0, table[0:1, :], 0.0)
    for i in range(1, table.shape[0]):
        value = jnp.where(column == float(i), table[i : i + 1, :], value)
    return value


def fused_kernel(
    tokens,
    languages,
    lang_group,
    group_gain,
    group_b2,
    b1,
    gain2,
    sb1,
    sb2,
    w1_hbm,
    w2_hbm,
    sw1_hbm,
    sw2_hbm,
    encoded,
    w1,
    w2,
    sw1,
    sw2,
    outgoing,
    rows_a,
    part_a,
    rs_a,
    ret_a,
    rows_b,
    part_b,
    rs_b,
    ret_b,
    hidden,
    sgather,
    shidden,
    spart,
    sown,
    scross,
    ssum,
    middle,
    sgather_b,
    shidden_b,
    spart_b,
    sown_b,
    scross_b,
    ssum_b,
    middle_b,
    back_a,
    back_b,
    compact,
    spread,
    w_sem,
    local_sem,
    disp_send,
    disp_recv,
    g_send,
    g_recv,
    r_send,
    r_recv,
    ret_send,
    ret_recv,
    sg_send,
    sg_recv,
    sr_send,
    sr_recv,
):
    bf16, f32 = jnp.bfloat16, jnp.float32
    g = lax.axis_index("group")
    w = lax.axis_index("within")
    x, z = lax.rem(w, 2), lax.div(w, 2)
    p = z + x * (7 - 2 * z)

    def device_at(q):
        q = lax.rem(q + 8, 8)
        far = lax.div(q, 4)
        return 2 * q + far * (15 - 4 * q)

    right = (g, device_at(p + 1))
    left = (g, device_at(p - 1))
    yy, core = lax.div(g, 2), lax.rem(g, 2)
    peers = [
        None,
        (2 * yy + 1 - core, w),
        (2 * (1 - yy) + core, w),
        (2 * (1 - yy) + 1 - core, w),
    ]
    barrier = pltpu.get_barrier_semaphore()
    for device in (right, left, peers[1], peers[2], peers[3]):
        pl.semaphore_signal(barrier, inc=1, device_id=device, device_id_type=MESH)

    loads = []
    for i, (src, dst) in enumerate(
        ((w1_hbm, w1), (w2_hbm, w2), (sw1_hbm, sw1), (sw2_hbm, sw2))
    ):
        copy = pltpu.make_async_copy(src, dst, w_sem.at[i])
        copy.start()
        loads.append(copy)

    count = tokens.shape[0]
    cap_a, cap_b = count // 4, count // 8
    late = count // 4
    i0 = lax.broadcasted_iota(jnp.int32, (count, count), 0)
    i1 = lax.broadcasted_iota(jnp.int32, (count, count), 1)
    eye = i0 == i1

    def to_column(row):
        return jnp.sum(jnp.where(eye, row, 0.0), axis=1, keepdims=True)

    def to_row(column):
        return jnp.sum(jnp.where(eye, column, 0.0), axis=0, keepdims=True)

    num_langs = lang_group.shape[1]
    lang = to_column(languages[...].astype(f32))
    lang_ids = lax.broadcasted_iota(jnp.int32, (count, num_langs), 1).astype(f32)
    group_column = jnp.sum(
        jnp.where(lang == lang_ids, lang_group[...].astype(f32), 0.0), axis=1, keepdims=True
    )
    group_row = to_row(group_column)
    same = group_column == group_row
    slot_column = row_sum(same & (i1 < i0))
    slot_row = column_sum(same & (i0 < i1))
    my_y, my_core = yy.astype(f32), core.astype(f32)

    def position(group, slot):
        gy = jnp.where(group >= 2.0, 1.0, 0.0)
        dy, dc = gy - my_y, group - 2.0 * gy - my_core
        r = 2.0 * dy * dy + dc * dc
        return jnp.where(
            slot < cap_a, r * cap_a + slot, count + r * cap_b + slot - cap_a
        )

    place_column = position(group_column, slot_column)
    place_row = position(group_row, slot_row)
    total_slots = 4 * (cap_a + cap_b)
    out_map = (
        lax.broadcasted_iota(jnp.int32, (total_slots, count), 0).astype(f32) == place_row
    )
    normed = layer_norm(
        tokens[...].astype(f32), by_group(group_column, group_gain)
    ).astype(bf16)
    outgoing[...] = jnp.dot(
        jnp.where(out_map, 1.0, 0.0).astype(bf16), normed, preferred_element_type=f32
    ).astype(bf16)
    base = {"a": 0, "b": 4 * cap_a}
    caps = {"a": cap_a, "b": cap_b}
    stage = {"a": 0, "b": 1}
    rows = {"a": rows_a, "b": rows_b}
    part = {"a": part_a, "b": part_b}
    rs = {"a": rs_a, "b": rs_b}
    ret = {"a": ret_a, "b": ret_b}
    own = {}
    for k in "ab":
        own[k] = pltpu.make_async_copy(
            outgoing.at[pl.ds(base[k], caps[k])],
            rows[k].at[pl.ds(0, caps[k])],
            local_sem.at[stage[k]],
        )
        own[k].start()
    pl.semaphore_wait(barrier, 5)

    pending = []

    def send(src, dst, send_sem, recv_sem, device):
        copy = pltpu.make_async_remote_copy(
            src_ref=src,
            dst_ref=dst,
            send_sem=send_sem,
            recv_sem=recv_sem,
            device_id=device,
            device_id_type=MESH,
        )
        copy.start()
        pending.append(copy)
        return copy

    def drain(keep):
        while len(pending) > keep:
            pending.pop(0).wait_send()

    def chunk(k, slot, c):
        return pl.ds((slot * 4 + c) * caps[k], caps[k])

    dispatch = {}
    for k in "ab":
        for r in (2, 3, 1):
            dispatch[k, r] = send(
                outgoing.at[pl.ds(base[k] + r * caps[k], caps[k])],
                rows[k].at[chunk(k, 0, r)],
                disp_send.at[stage[k], r],
                disp_recv.at[stage[k], r],
                peers[r],
            )

    def slot_of(way, s):
        return 7 if s == 4 else (0 if s == 0 else 2 * s - 1 + way)

    arrivals = {}

    def forward(k, way, s, c):
        arrivals[k, way, s + 1, c] = send(
            rows[k].at[chunk(k, slot_of(way, s), c)],
            rows[k].at[chunk(k, slot_of(way, s + 1), c)],
            g_send.at[stage[k], way, s, c],
            g_recv.at[stage[k], way, s + 1, c],
            right if way == 0 else left,
        )

    def first_tiles(k, slot, slots, begin, end):
        size = slots * 4 * caps[k]

        def body(i, carry):
            cols = columns(i, TILE)
            value = jnp.dot(
                rows[k][pl.ds(slot * 4 * caps[k], size), :],
                w1[:, cols],
                preferred_element_type=f32,
            )
            hidden[pl.ds(0, size), cols] = jnp.maximum(value + b1[:, cols], 0.0).astype(bf16)
            return carry

        lax.fori_loop(begin, end, body, 0)

    def second_tiles(k, slot, slots, begin, end):
        size = slots * 4 * caps[k]

        def body(i, carry):
            cols = columns(i, TILE)
            part[k][pl.ds(slot * 4 * caps[k], size), cols] = jnp.dot(
                hidden[pl.ds(0, size), :], w2[:, cols], preferred_element_type=f32
            ).astype(bf16)
            return carry

        lax.fori_loop(begin, end, body, 0)

    n1, n2 = w1.shape[1] // TILE, w2.shape[1] // TILE

    def piece(k, slot, slots, c):
        if c < 2:
            first_tiles(k, slot, slots, c * n1 // 2, (c + 1) * n1 // 2)
        else:
            second_tiles(k, slot, slots, (c - 2) * n2 // 2, (c - 1) * n2 // 2)

    def whole(k, slot, slots):
        first_tiles(k, slot, slots, 0, n1)
        second_tiles(k, slot, slots, 0, n2)

    def gather_start(k):
        own[k].wait()
        for c in range(4):
            if c:
                dispatch[k, c].wait_recv()
            forward(k, 0, 0, c)
            forward(k, 1, 0, c)

    def gather_step(k, s, c):
        for way in (0, 1):
            arrivals[k, way, s, c].wait_recv()
            if s < 3 or c // 2 == way:
                forward(k, way, s, c)

    def rs_slot(way, t):
        return (7, 6 - way, 4 - way, 2 - way)[t]

    def rs_chunk(k, way, t, c):
        at = way * 14 + (c % 2 if t == 0 else 4 * t - 2 + c)
        return pl.ds(at * caps[k], caps[k])

    sums = {}

    def pass_on(k, way, t, c):
        sums[k, way, t, c] = send(
            part[k].at[chunk(k, rs_slot(way, t), c)],
            rs[k].at[rs_chunk(k, way, t, c)],
            r_send.at[stage[k], way, t, c],
            r_recv.at[stage[k], way, t, c],
            right if way == 0 else left,
        )

    def add_in(k, way, t, c):
        sums[k, way, t, c].wait_recv()
        here = chunk(k, rs_slot(way, t + 1), c)
        part[k][here, :] = (
            part[k][here, :].astype(f32) + rs[k][rs_chunk(k, way, t, c), :].astype(f32)
        ).astype(bf16)
        pass_on(k, way, t + 1, c)

    order = (2, 3, 0, 1)

    def reduce_start(k, between):
        for c in (2, 3):
            pass_on(k, 0, 1, c)
            pass_on(k, 1, 1, c - 2)
        between()
        for c in (0, 1):
            arrivals[k, 0, 4, c].wait_recv()
            arrivals[k, 1, 4, c + 2].wait_recv()
        whole(k, 7, 1)
        for c in (0, 1):
            pass_on(k, 0, 0, c)
            pass_on(k, 1, 0, c + 2)
        between()
        for c in (0, 1):
            add_in(k, 0, 0, c)
            add_in(k, 1, 0, c + 2)

    returned = {}

    def reduce_end(k, c):
        sums[k, 0, 3, c].wait_recv()
        sums[k, 1, 3, c].wait_recv()
        here = chunk(k, 0, c)
        total = (
            part[k][here, :].astype(f32)
            + rs[k][rs_chunk(k, 0, 3, c), :].astype(f32)
            + rs[k][rs_chunk(k, 1, 3, c), :].astype(f32)
        ).astype(bf16)
        if c == 0:
            ret[k][pl.ds(0, caps[k]), :] = total
        else:
            part[k][here, :] = total
            returned[k, c] = send(
                part[k].at[here],
                ret[k].at[pl.ds(c * caps[k], caps[k])],
                ret_send.at[stage[k], c],
                ret_recv.at[stage[k], c],
                peers[c],
            )

    m1, m2 = sw1.shape[1] // TILE, sw2.shape[1] // TILE

    def shared_first(source, start, size, target, begin, end):
        def body(i, carry):
            cols = columns(i, TILE)
            value = jnp.dot(
                source[pl.ds(start, size), :], sw1[:, cols], preferred_element_type=f32
            )
            target[:, cols] = jnp.maximum(value + sb1[:, cols], 0.0).astype(bf16)
            return carry

        lax.fori_loop(begin, end, body, 0)

    def shared_second(source, target, start, size, begin, end):
        def body(i, carry):
            cols = columns(i, TILE)
            target[pl.ds(start, size), cols] = jnp.dot(
                source[...], sw2[:, cols], preferred_element_type=f32
            ).astype(bf16)
            return carry

        lax.fori_loop(begin, end, body, 0)

    quarters = 4
    width = sw2.shape[1] // quarters

    def quarter(q):
        return pl.ds(q * width, width)

    def add_crossed(source, cross, target, at, copy, send_sem, recv_sem, q):
        cols = quarter(q)
        copy.wait_recv()
        source[at, cols] = (
            source[at, cols].astype(f32) + cross[:, cols].astype(f32)
        ).astype(bf16)
        return send(source.at[at, cols], target.at[:, cols], send_sem, recv_sem, peers[2])

    def combined(total, own_part, sibling, crossed, cols):
        return (
            total
            + (own_part.astype(f32) + sibling.astype(f32) + crossed.astype(f32))
            + sb2[:, cols]
        )

    half = count // 2

    def block(r, h=None):
        if h is None:
            return pl.ds(r * count, count)
        return pl.ds(r * count + h * half, half)

    def shared_a():
        for c in (1, 2, 3):
            returned["a", c].wait_recv()
        from_sibling, from_y, from_far = [], [], []
        for h in range(2):
            some = pl.ds(h * half, half)
            value = middle[some, :] + jnp.dot(
                back_a[some, :], ret_a[...], preferred_element_type=f32
            )
            middle[some, :] = value
            sgather[some, :] = layer_norm(value, gain2[...]).astype(bf16)
            for r, into in ((2, from_y), (1, from_sibling)):
                into.append(
                    send(
                        sgather.at[some],
                        sgather.at[block(r, h)],
                        sg_send.at[r, h],
                        sg_recv.at[r, h],
                        peers[r],
                    )
                )
        yield
        loads[2].wait()
        loads[3].wait()
        for h in range(2):
            from_sibling[h].wait_recv()
        for q in range(4):
            shared_first(sgather, 0, 2 * count, shidden, q * m1 // 4, (q + 1) * m1 // 4)
            yield
        for q in range(4):
            shared_second(shidden, spart, 0, 2 * count, q * m2 // 4, (q + 1) * m2 // 4)
            yield
        to_own = send(
            spart.at[block(1)], sown, sr_send.at[2, 0], sr_recv.at[2, 0], peers[1]
        )
        yield
        for h in range(2):
            from_y[h].wait_recv()
            from_far.append(
                send(
                    sgather.at[block(2, h)],
                    sgather.at[block(3, h)],
                    sg_send.at[3, h],
                    sg_recv.at[3, h],
                    peers[1],
                )
            )
            yield
        for h in range(2):
            from_far[h].wait_recv()
        for q in range(4):
            shared_first(
                sgather, 2 * count, 2 * count, shidden, q * m1 // 4, (q + 1) * m1 // 4
            )
            yield
        crossed, summed = [], []

        def finish(q):
            summed.append(
                add_crossed(
                    spart, scross, ssum, block(2), crossed[q], sr_send.at[1, q], sr_recv.at[1, q], q
                )
            )

        for q in range(quarters):
            shared_second(
                shidden, spart, 2 * count, 2 * count, q * m2 // 4, (q + 1) * m2 // 4
            )
            crossed.append(
                send(
                    spart.at[block(3), quarter(q)],
                    scross.at[:, quarter(q)],
                    sr_send.at[0, q],
                    sr_recv.at[0, q],
                    peers[1],
                )
            )
            if q:
                finish(q - 1)
            yield
        finish(quarters - 1)
        yield
        to_own.wait_recv()
        for q in range(quarters):
            cols = quarter(q)
            summed[q].wait_recv()
            middle[:, cols] = combined(
                middle[:, cols], spart[block(0), cols], sown[:, cols], ssum[:, cols], cols
            )
            yield

    gather_start("a")
    back_a[...] = jnp.where(
        lax.broadcasted_iota(jnp.int32, (count, 4 * cap_a), 1).astype(f32) == place_column,
        1.0,
        0.0,
    ).astype(bf16)
    middle[...] = tokens[...].astype(f32) + by_group(group_column, group_b2)
    rank_row = column_sum((slot_column >= cap_a) & (i0 < i1))
    rank_row = jnp.where(slot_row >= cap_a, rank_row, -1.0)
    rank_column = row_sum((slot_row >= cap_a) & (i1 < i0))
    rank_column = jnp.where(slot_column >= cap_a, rank_column, -1.0)
    pick = jnp.where(
        lax.broadcasted_iota(jnp.int32, (late, count), 0).astype(f32) == rank_row, 1.0, 0.0
    )
    compact[...] = pick.astype(bf16)
    spread[...] = jnp.where(
        lax.broadcasted_iota(jnp.int32, (count, late), 1).astype(f32) == rank_column, 1.0, 0.0
    ).astype(bf16)
    late_place = jnp.sum(pick * place_row, axis=1, keepdims=True) - 4.0 * cap_a
    late_group = jnp.sum(pick * group_row, axis=1, keepdims=True)
    back_b[...] = jnp.where(
        lax.broadcasted_iota(jnp.int32, (late, 4 * cap_b), 1).astype(f32) == late_place,
        1.0,
        0.0,
    ).astype(bf16)
    middle_b[...] = jnp.dot(
        compact[...], tokens[...], preferred_element_type=f32
    ) + by_group(late_group, group_b2)
    loads[0].wait()
    loads[1].wait()
    for s in (1, 2, 3):
        for c in range(4):
            gather_step("a", s, c)
            if s == 1:
                piece("a", 0, 1, c)
            else:
                piece("a", 2 * s - 3, 2, c)
    whole("a", 5, 2)
    reduce_start("a", lambda: None)
    for t in (1, 2):
        for c in order:
            for way in (0, 1):
                add_in("a", way, t, c)

    gather_start("b")
    for c in order:
        reduce_end("a", c)
    shared = shared_a()

    def go_on():
        next(shared, None)

    for s in (1, 2, 3):
        for c in range(4):
            gather_step("b", s, c)
            if s == 3:
                piece("b", 0, 5, c)
            go_on()
    whole("b", 5, 2)
    reduce_start("b", go_on)
    for t in (1, 2):
        for c in order:
            for way in (0, 1):
                add_in("b", way, t, c)
            go_on()
    for c in order:
        reduce_end("b", c)
        go_on()
    for _ in shared:
        pass

    for c in (1, 2, 3):
        returned["b", c].wait_recv()

    def block_b(r):
        return pl.ds(r * late, late)

    value = middle_b[...] + jnp.dot(back_b[...], ret_b[...], preferred_element_type=f32)
    middle_b[...] = value
    sgather_b[block_b(0), :] = layer_norm(value, gain2[...]).astype(bf16)
    near = {}
    for r in (2, 1):
        near[r] = send(
            sgather_b.at[block_b(0)],
            sgather_b.at[block_b(r)],
            sg_send.at[r, 2],
            sg_recv.at[r, 2],
            peers[r],
        )
    drain(8)
    near[2].wait_recv()
    near[3] = send(
        sgather_b.at[block_b(2)],
        sgather_b.at[block_b(3)],
        sg_send.at[3, 2],
        sg_recv.at[3, 2],
        peers[1],
    )
    near[1].wait_recv()
    near[3].wait_recv()
    shared_first(sgather_b, 0, 4 * late, shidden_b, 0, m1)
    crossed, to_own, summed = [], [], []

    def finish_b(q):
        summed.append(
            add_crossed(
                spart_b,
                scross_b,
                ssum_b,
                block_b(2),
                crossed[q],
                sr_send.at[4, q],
                sr_recv.at[4, q],
                q,
            )
        )

    for q in range(quarters):
        cols = quarter(q)
        shared_second(shidden_b, spart_b, 0, 4 * late, q * m2 // 4, (q + 1) * m2 // 4)
        crossed.append(
            send(
                spart_b.at[block_b(3), cols],
                scross_b.at[:, cols],
                sr_send.at[3, q],
                sr_recv.at[3, q],
                peers[1],
            )
        )
        to_own.append(
            send(
                spart_b.at[block_b(1), cols],
                sown_b.at[:, cols],
                sr_send.at[5, q],
                sr_recv.at[5, q],
                peers[1],
            )
        )
        if q:
            finish_b(q - 1)
    finish_b(quarters - 1)
    is_late = jnp.sum(spread[...].astype(f32), axis=1, keepdims=True)
    for q in range(quarters):
        cols = quarter(q)
        to_own[q].wait_recv()
        summed[q].wait_recv()
        late_out = combined(
            middle_b[:, cols], spart_b[block_b(0), cols], sown_b[:, cols], ssum_b[:, cols], cols
        ).astype(bf16)
        placed = jnp.dot(spread[...], late_out, preferred_element_type=f32)
        encoded[:, cols] = jnp.where(is_late > 0.5, placed, middle[:, cols]).astype(bf16)
    drain(0)


def fused_on_device(
    tokens,
    languages,
    lang_group,
    group_gain,
    group_w1,
    group_b1,
    group_w2,
    group_b2,
    shared_gain,
    shared_w1,
    shared_b1,
    shared_w2,
    shared_b2,
):
    count, width = tokens.shape
    unit = group_w1.shape[2]
    shared_unit = shared_w1.shape[1]
    cap_a, cap_b = count // 4, count // 8
    late = count // 4
    bf16, f32 = jnp.bfloat16, jnp.float32
    in_vmem = pl.BlockSpec(memory_space=pltpu.VMEM)
    anywhere = pl.BlockSpec(memory_space=pl.ANY)
    dma = pltpu.SemaphoreType.DMA

    def held(rows, columns=width, dtype=bf16):
        return pltpu.VMEM((rows, columns), dtype)

    return pl.pallas_call(
        fused_kernel,
        out_shape=jax.ShapeDtypeStruct((count, width), bf16),
        in_specs=[in_vmem] * 9 + [anywhere] * 4,
        out_specs=in_vmem,
        scratch_shapes=[
            held(width, unit),
            held(unit),
            held(width, shared_unit),
            held(shared_unit),
            held(4 * (cap_a + cap_b)),
            held(32 * cap_a),
            held(32 * cap_a),
            held(28 * cap_a),
            held(4 * cap_a),
            held(32 * cap_b),
            held(32 * cap_b),
            held(28 * cap_b),
            held(4 * cap_b),
            held(max(8 * cap_a, 20 * cap_b), unit),
            held(4 * count),
            held(2 * count, shared_unit),
            held(4 * count),
            held(count),
            held(count),
            held(count),
            held(count, dtype=f32),
            held(4 * late),
            held(4 * late, shared_unit),
            held(4 * late),
            held(late),
            held(late),
            held(late),
            held(late, dtype=f32),
            held(count, 4 * cap_a),
            held(late, 4 * cap_b),
            held(late, count),
            held(count, late),
            dma((4,)),
            dma((2,)),
            dma((2, 4)),
            dma((2, 4)),
            dma((2, 2, 4, 4)),
            dma((2, 2, 5, 4)),
            dma((2, 2, 4, 4)),
            dma((2, 2, 4, 4)),
            dma((2, 4)),
            dma((2, 4)),
            dma((4, 3)),
            dma((4, 3)),
            dma((6, 4)),
            dma((6, 4)),
        ],
        compiler_params=pltpu.CompilerParams(
            collective_id=0, has_side_effects=True, vmem_limit_bytes=62 * 1024 * 1024
        ),
    )(
        tokens,
        languages[None, :],
        lang_group[None, :],
        group_gain,
        group_b2,
        group_b1,
        shared_gain[None, :],
        shared_b1[None, :],
        shared_b2[None, :],
        group_w1[0],
        group_w2[0],
        shared_w1,
        shared_w2,
    )


def plain_on_device(
    tokens,
    languages,
    lang_group,
    group_gain,
    group_w1,
    group_b1,
    group_w2,
    group_b2,
    shared_gain,
    shared_w1,
    shared_b1,
    shared_w2,
    shared_b2,
):
    tok_dev = tokens.shape[0]
    width_model = tokens.shape[1]
    num_groups = group_gain.shape[0]
    num_langs = lang_group.shape[0]
    capacity = 3 * tok_dev // (2 * lax.axis_size("group"))
    residual_in = tokens.astype(jnp.float32)
    lang_hit = (languages[:, None] == jnp.arange(num_langs, dtype=jnp.int32)[None, :]).astype(
        jnp.int32
    )
    group_of = jnp.sum(lang_hit * lang_group[None, :], axis=1)
    onehot = (group_of[:, None] == jnp.arange(num_groups, dtype=jnp.int32)[None, :]).astype(
        jnp.int32
    )
    earlier = jnp.cumsum(onehot, axis=0) - onehot
    slot_index = jnp.sum(earlier * onehot, axis=1)
    position = group_of * capacity + slot_index
    dispatch_map = (
        position[None, :] == jnp.arange(num_groups * capacity, dtype=jnp.int32)[:, None]
    ).astype(jnp.bfloat16)
    onehot_float = onehot.astype(jnp.float32)
    row_gains = jnp.dot(onehot_float, group_gain, precision=lax.Precision.HIGHEST)
    normed = layer_norm(residual_in, row_gains).astype(jnp.bfloat16)
    outgoing = jnp.dot(dispatch_map, normed, preferred_element_type=jnp.float32).astype(
        jnp.bfloat16
    )
    outgoing = outgoing.reshape(num_groups, capacity, width_model)
    arrived = lax.all_to_all(outgoing, "group", split_axis=0, concat_axis=0, tiled=True)
    group_rows = arrived.reshape(num_groups * capacity, width_model)
    first_proj = group_w1[0]
    first_bias = group_b1[0]
    second_proj = group_w2[0]
    hidden = jax.nn.relu(
        jnp.dot(
            lax.all_gather(group_rows, "within", axis=0, tiled=True),
            first_proj,
            preferred_element_type=jnp.float32,
        )
        + first_bias
    ).astype(jnp.bfloat16)
    selected = hidden
    summed = lax.psum_scatter(
        jnp.dot(selected, second_proj, preferred_element_type=jnp.float32).astype(jnp.bfloat16),
        "within",
        scatter_dimension=0,
        tiled=True,
    )
    returned = lax.all_to_all(
        summed.reshape(num_groups, capacity, width_model),
        "group",
        split_axis=0,
        concat_axis=0,
        tiled=True,
    )
    returned = returned.reshape(num_groups * capacity, width_model)
    group_out = lax.dot_general(
        dispatch_map, returned, (((0,), (0,)), ((), ())), preferred_element_type=jnp.float32
    )
    group_bias = jnp.dot(onehot_float, group_b2, precision=lax.Precision.HIGHEST)
    middle = residual_in + group_out + group_bias
    shared_in = layer_norm(middle, shared_gain).astype(jnp.bfloat16)
    shared_hidden = jax.nn.relu(
        jnp.dot(
            lax.all_gather(shared_in, "group", axis=0, tiled=True),
            shared_w1,
            preferred_element_type=jnp.float32,
        )
        + shared_b1
    ).astype(jnp.bfloat16)
    selected = shared_hidden
    shared_out = lax.psum_scatter(
        jnp.dot(selected, shared_w2, preferred_element_type=jnp.float32).astype(jnp.bfloat16),
        "group",
        scatter_dimension=0,
        tiled=True,
    ).astype(jnp.float32)
    return (middle + shared_out + shared_b2).astype(jnp.bfloat16)


def solution(mesh):
    placed = (
        P(("group", "within"), None),
        P(("group", "within")),
        P(),
        P(),
        P("group", None, "within"),
        P("group", "within"),
        P("group", "within", None),
        P(),
        P(),
        P(None, "group"),
        P("group"),
        P("group", None),
        P(),
    )
    fits = mesh.shape["group"] == 4 and mesh.shape["within"] == 8
    return jax.shard_map(
        fused_on_device if fits else plain_on_device,
        mesh=mesh,
        in_specs=placed,
        out_specs=P(("group", "within"), None),
        check_vma=False,
    )
```
